512 devices in a mesh: row: 8 (over y, x_hi), col: 16 (over z), depth: 4 (over x_lo, core).
Axes of the slice: x: 4 (x_hi: 2, x_lo: 2; x = x_hi * 2 + x_lo), y: 4, z: 16, core: 2. Of those that a mesh axis runs over, the one named last changes fastest.
Arguments:
- feats: bfloat16 [65536, 256], P(('row', 'col', 'depth')), may hold values from -6 to 6
- tile_values: bfloat16 [8, 16, 4, 96, 128, 128], P('row', 'col', 'depth'), may hold values from 0.0049743652 to 0.049804688
- tile_rows: int32 [8, 16, 4, 96], P('row', 'col', 'depth'), may hold values from 0 to 15
- tile_cols: int32 [8, 16, 4, 96], P('row', 'col', 'depth'), may hold values from 0 to 31
- tile_count: int32 [8, 16, 4], P('row', 'col', 'depth'), may hold values from 1 to 96, as said below
- weight: bfloat16 [256, 256], replicated, may hold values from -0.375 to 0.375
- cotangent: bfloat16 [65536, 256], P(('row', 'col', 'depth')), may hold values from -6 to 6
Outputs:
- hidden: bfloat16 [65536, 256], P(('row', 'col', 'depth'))
- grad_feats: bfloat16 [65536, 256], P(('row', 'col', 'depth'))
- grad_weight: float32 [256, 256], replicated
The draws below stay inside these ranges and needn't reach their ends.
Inputs may be any that keep to these rules, and one draw needn't show every extreme that they name: `tile_count`: every cell has at least one live slot; in each grid column j, every cell (i, j, l) with i = j * 8 div 16 (for all l) has all 96 slots live.
All inputs are finite; a program needn't handle non-finite values.
Results may differ from the reference program's by a relative error of at most 0.03.
Values may be sent and summed in bfloat16 or wider, within the bound.
A program may use at most 128 MiB of HBM per device.

```python
import math
import jax
import jax.numpy as jnp
from jax import lax

F = 256
TILE = 128
TILES = 96
GRID_ROW = 8
MESH_SECOND_SPAN = 16
GRID_DEPTH = 4
NODES = 65536


def draw_tile_count(key, part):
    key = jax.random.fold_in(key, 7)
    shape = (GRID_ROW, MESH_SECOND_SPAN, GRID_DEPTH)
    base = jax.random.randint(key, shape, TILES // 4, TILES // 2 + 1)
    row_index = lax.broadcasted_iota(jnp.int32, shape, 0)
    col_index = lax.broadcasted_iota(jnp.int32, shape, 1)
    diagonal = row_index == col_index * GRID_ROW // MESH_SECOND_SPAN
    return jnp.where(diagonal, TILES, base).astype(jnp.int32)


def plant(values, key, smallest, high):
    longest = values.shape.index(max(values.shape))
    spots = []
    for shift in (0, 1):
        where = [jax.random.randint(jax.random.fold_in(key, axis), (), 0, length) for axis, length in enumerate(values.shape)]
        where[longest] = (where[longest] + shift) % values.shape[longest]
        spots.append(tuple(where))
    return values.at[spots[0]].set(smallest).at[spots[1]].set(high)


def shard_levels(stream_key, extent, split, least, high):
    loudness, own = 1.0, jax.random.fold_in(stream_key, 6)
    for axis_at, blocks in split:
        steps = jnp.exp(jax.random.uniform(jax.random.fold_in(own, axis_at), (blocks,), jnp.float32, least / len(split), high / len(split)))
        loudness = loudness * jnp.repeat(steps, extent[axis_at] // blocks).reshape([-1 if axis == axis_at else 1 for axis in range(len(extent))])
    return loudness


def bell_draw(rng, shape, spread, bound, split=(), held_as=jnp.bfloat16):
    factor_of = shard_levels(rng, shape, split, -0.22, 0.18) if split else 1.0
    result = jax.random.normal(rng, shape, jnp.float32) * spread * factor_of
    return jnp.minimum(jnp.maximum(result, -bound), bound).astype(held_as)


def setup_inputs(seed: int = 0) -> dict:
    seeds = jax.random.split(jax.random.key(seed), 8)
    feats = bell_draw(seeds[0], (NODES, F), 1.0, 6.0, ((0, 512),))
    tile_values = jnp.clip(jnp.exp(math.log(0.049804688) - 2.3038113 * jax.random.uniform(seeds[1], (GRID_ROW, MESH_SECOND_SPAN, GRID_DEPTH, TILES, TILE, TILE), jnp.float32) ** shard_levels(seeds[1], (GRID_ROW, MESH_SECOND_SPAN, GRID_DEPTH, TILES, TILE, TILE), ((0, 8), (1, 16), (2, 4)), -0.2, 0.2)), 0.0049743652, 0.049804688).astype(jnp.bfloat16)
    tile_rows = plant(jax.random.randint(seeds[2], (GRID_ROW, MESH_SECOND_SPAN, GRID_DEPTH, TILES), 0, MESH_SECOND_SPAN), jax.random.fold_in(seeds[2], 1), 0, MESH_SECOND_SPAN - 1).astype(jnp.int32)
    tile_cols = plant(jax.random.randint(seeds[3], (GRID_ROW, MESH_SECOND_SPAN, GRID_DEPTH, TILES), 0, GRID_ROW * GRID_DEPTH), jax.random.fold_in(seeds[3], 1), 0, (GRID_ROW * GRID_DEPTH) - 1).astype(jnp.int32)
    tile_count = draw_tile_count(jax.random.fold_in(seeds[7], 71), 0)
    weight = bell_draw(seeds[5], (F, F), F ** -0.5, 0.375)
    cotangent = bell_draw(seeds[6], (NODES, F), 1.0, 6.0, ((0, 512),))
    return {"feats": feats, "tile_values": tile_values, "tile_rows": tile_rows, "tile_cols": tile_cols, "tile_count": tile_count, "weight": weight, "cotangent": cotangent}


def reference(feats, tile_values, tile_rows, tile_cols, tile_count, weight, cotangent):
    first_grid_axis, grid_two, mesh_third_extent = tile_count.shape
    width = feats.shape[1]
    tile_size = tile_values.shape[-1]
    slots = tile_values.shape[3]
    cells = first_grid_axis * grid_two * mesh_third_extent
    flat_vals = tile_values.reshape(cells, slots, tile_size, tile_size)
    flat_rows = tile_rows.reshape(cells, slots).astype(jnp.int32)
    flat_cols = tile_cols.reshape(cells, slots).astype(jnp.int32)
    flat_count = tile_count.reshape(cells).astype(jnp.int32)
    position_number = jnp.arange(slots, dtype=jnp.int32)
    row_interval = jnp.arange(grid_two, dtype=jnp.int32)
    col_range = jnp.arange(first_grid_axis * mesh_third_extent, dtype=jnp.int32)
    cell_index = jnp.arange(cells, dtype=jnp.int32)
    source = feats.astype(jnp.float32).reshape(first_grid_axis, grid_two, mesh_third_extent, tile_size, width)

    def locate(index):
        return index // (grid_two * mesh_third_extent), (index // mesh_third_extent) % grid_two, index % mesh_third_extent

    def quantized_result(value):
        return lax.optimization_barrier(value.astype(jnp.bfloat16)).astype(jnp.float32)

    def forward_step(accumulated_total, index):
        outer, middle, inner = locate(index)
        tiles = flat_vals[index].astype(jnp.float32)
        live = (position_number < flat_count[index]).astype(jnp.float32)
        columns = flat_cols[index]
        picked = source[columns // mesh_third_extent, middle, columns % mesh_third_extent]
        products = jnp.einsum("kab,kbf->kaf", tiles, picked)
        indicator_matrix = (flat_rows[index][:, None] == row_interval[None, :]).astype(jnp.float32) * live[:, None]
        entry_fraction = jnp.einsum("kt,kaf->taf", indicator_matrix, products, precision=lax.Precision.HIGHEST)
        accumulated_total = accumulated_total.at[outer, :, inner].add(quantized_result(entry_fraction))
        return accumulated_total, None

    start = jnp.zeros((first_grid_axis, grid_two, mesh_third_extent, tile_size, width), jnp.float32)
    accumulated_total, _ = lax.scan(forward_step, start, cell_index)
    aggregated = accumulated_total.reshape(NODES, width).astype(jnp.bfloat16)
    preact = jnp.dot(aggregated, weight, preferred_element_type=jnp.float32)
    sigma = jax.nn.sigmoid(preact)
    hidden = (preact * sigma).astype(jnp.bfloat16)
    derivative_before_activation = (cotangent.astype(jnp.float32) * sigma * (1.0 + preact * (1.0 - sigma))).astype(jnp.bfloat16)
    grad_weight = jnp.dot(aggregated.T, derivative_before_activation, preferred_element_type=jnp.float32) * (NODES ** -0.5)
    grad_agg = jnp.dot(derivative_before_activation, weight.T, preferred_element_type=jnp.float32).astype(jnp.bfloat16)
    grad_src = grad_agg.astype(jnp.float32).reshape(first_grid_axis, grid_two, mesh_third_extent, tile_size, width)

    def backward_step(accumulated_total, index):
        outer, middle, inner = locate(index)
        tiles = flat_vals[index].astype(jnp.float32)
        live = (position_number < flat_count[index]).astype(jnp.float32)
        fetched = grad_src[outer, :, inner][flat_rows[index]]
        contribution = jnp.einsum("kab,kaf->kbf", tiles, fetched)
        indicator_matrix = (flat_cols[index][:, None] == col_range[None, :]).astype(jnp.float32) * live[:, None]
        entry_fraction = jnp.einsum("an,arp->nrp", indicator_matrix, contribution, precision=lax.Precision.HIGHEST)
        entry_fraction = quantized_result(entry_fraction).reshape(first_grid_axis, mesh_third_extent, tile_size, width)
        accumulated_total = accumulated_total.at[:, middle].add(entry_fraction)
        return accumulated_total, None

    back, _ = lax.scan(backward_step, start, cell_index)
    grad_feats = back.reshape(NODES, width).astype(jnp.bfloat16)
    return hidden, grad_feats, grad_weight
```

```python
import jax
import jax.numpy as jnp
from jax import lax
from jax.experimental import pallas as pl
from jax.experimental.pallas import tpu as pltpu
from jax.sharding import PartitionSpec as P

MESH = pl.DeviceIdType.MESH
BF, F32 = jnp.bfloat16, jnp.float32

NX, NY, NZ = 4, 4, 16
TILE, F, SLOTS = 128, 256, 96
NROWS, NCOLS = NZ, NX * NY * 2
FPOS, BPOS = SLOTS + NROWS, SLOTS + NCOLS
FPAIRS, BPAIRS = FPOS // 2, BPOS // 2
Q = 4
REL = (2, 1, 3, 0)

F_IDX, F_OTH = 0, FPOS
F_KEEP = F_OTH + FPOS
F_LAST = F_KEEP + FPAIRS
B_IDX = F_LAST + NROWS
B_OTH = B_IDX + BPOS
B_KEEP = B_OTH + BPOS
B_LAST = B_KEEP + BPAIRS
TABLE = B_LAST + NCOLS


def schedule(key, other, live, keys, other_zero):
    slots = key.shape[0]
    positions = slots + keys
    hot = (key[:, None] == lax.iota(jnp.int32, keys)[None, :]) & live[:, None]
    hot_i = hot.astype(jnp.int32)
    count = jnp.sum(hot_i, axis=0)
    padded = (count + 1) // 2 * 2
    before = lax.iota(jnp.int32, keys)[:, None] < lax.iota(jnp.int32, keys)[None, :]
    start = jnp.sum(jnp.where(before, padded[:, None], 0), axis=0)
    earlier = lax.iota(jnp.int32, slots)[:, None] < lax.iota(jnp.int32, slots)[None, :]
    same = (key[:, None] == key[None, :]) & live[:, None] & earlier
    rank = jnp.sum(same.astype(jnp.int32), axis=0)
    place = jnp.sum(hot_i * start[None, :], axis=1) + rank
    at = (place[:, None] == lax.iota(jnp.int32, positions)[None, :]) & live[:, None]
    slot = jnp.sum(jnp.where(at, lax.iota(jnp.int32, slots)[:, None], 0), axis=0)
    partner = jnp.sum(jnp.where(at, other[:, None] - other_zero, 0), axis=0) + other_zero
    pairs = positions // 2
    opens = (start[:, None] == 2 * lax.iota(jnp.int32, pairs)[None, :]) & (count > 0)[:, None]
    keep = 1 - jnp.sum(opens.astype(jnp.int32), axis=0)
    last = jnp.where(count > 0, (start + padded) // 2 - 1, pairs)
    return [slot, partner, keep, last]


def wait(ref, sem):
    pltpu.make_async_copy(ref, ref, sem).wait()


def kernel(
    table, feats, tiles, weight, cot, hidden_o, gf_o, gw_o,
    av, xg, fout, acc, wv, cv, zs, zr, gt, bout, sib_s, sib_r,
    d2s, d2r, d1s, d1r, vv, e2s, e2r, e1s, e1r, gft, gfv, hv,
    w1s, w1r, w2s, w2r, w3s, w3r, w4, w5, w6, w7, w8, lw, gwv,
    loc, ag_send, ag_recv, zs_send, zs_recv, zg_send, zg_recv,
    sb_send, sb_recv, rp_send, rp_recv, w_send, w_recv, out_sem,
):
    row, z, depth = lax.axis_index("row"), lax.axis_index("col"), lax.axis_index("depth")
    y, x, core = row // 2, (row % 2) * 2 + depth // 2, depth % 2

    def dev(dx=0, dy=0, dz=0, flip=0, zz=None):
        nx, ny = (x + dx) % NX, (y + dy) % NY
        nz = (z + dz + NZ) % NZ if zz is None else zz
        nc = (core + flip) % 2
        return {"row": ny * 2 + nx // 2, "col": nz, "depth": (nx % 2) * 2 + nc}

    def send(src, dst, ssem, rsem, to):
        pltpu.make_async_remote_copy(
            src_ref=src, dst_ref=dst, send_sem=ssem, recv_sem=rsem, device_id=to, device_id_type=MESH
        ).start()

    zi, zq = z % 4, z // 4
    partners = [dev(flip=1), dev(dz=1), dev(dz=-1)]
    for k in (1, 2, 3):
        partners += [dev(dx=k), dev(dy=k), dev(dz=4 * k), dev(zz=zq * 4 + (zi + k) % 4)]

    mine = 8 * y + 2 * x + core
    own_copy = pltpu.make_async_copy(feats, xg.at[mine], loc.at[0])
    own_copy.start()
    tile_copy = pltpu.make_async_copy(tiles, av, loc.at[1])
    tile_copy.start()
    weight_copy = pltpu.make_async_copy(weight, wv, loc.at[2])
    weight_copy.start()
    cot_copy = pltpu.make_async_copy(cot, cv, loc.at[3])
    cot_copy.start()

    barrier = pltpu.get_barrier_semaphore()
    for to in partners:
        pl.semaphore_signal(barrier, inc=1, device_id=to, device_id_type=MESH)
    pl.semaphore_wait(barrier, len(partners))

    xg[NCOLS] = jnp.zeros((TILE, F), BF)
    gt[NZ] = jnp.zeros((F, TILE), BF)
    fout[FPAIRS] = jnp.zeros((TILE, F), BF)
    bout[BPAIRS] = jnp.zeros((F, TILE), BF)

    def to_ab(h, da, db):
        return dev(dx=da, dy=db) if h == 0 else dev(dx=db, dy=da)

    def piece(h, da, db, flip=0):
        dx, dy = (da, db) if h == 0 else (db, da)
        return 8 * ((y + dy) % NY) + 2 * ((x + dx) % NX) + (core + flip) % 2

    def rows(h, part):
        if part is None:
            return pl.ds(64 * h, 64)
        return pl.ds(64 * h + 32 * part, 32)

    def xpart(h, da, db, part=None, flip=0):
        return xg.at[piece(h, da, db, flip), rows(h, part)]

    def forward(h, da, db, part, to, k, own=False):
        src = feats.at[rows(h, part)] if own else xpart(h, da, db, part)
        send(src, xpart(h, da, db, part), ag_send, ag_recv.at[h, k], to)

    def to_b(h, e, own=False):
        forward(h, e, 0, None, to_ab(h, 0, 1), 4 + e, own)
        forward(h, e, 0, None, to_ab(h, 0, 3), 8 + e, own)

    def to_sib(h, da, db, own=False):
        forward(h, da, db, None, dev(flip=1), 20 + 4 * da + db, own)

    for h in (0, 1):
        forward(h, 0, 0, None, to_ab(h, 1, 0), 0, True)
        forward(h, 0, 0, None, to_ab(h, 3, 0), 1, True)
    for h in (0, 1):
        to_b(h, 0, True)
        to_sib(h, 0, 0, True)
    for h in (0, 1):
        wait(xpart(h, 3, 0), ag_recv.at[h, 0])
        forward(h, 3, 0, 0, to_ab(h, 1, 0), 2)
        to_b(h, 3)
        wait(xpart(h, 1, 0), ag_recv.at[h, 1])
        forward(h, 1, 0, 1, to_ab(h, 3, 0), 3)
        to_b(h, 1)
        to_sib(h, 3, 0)
        to_sib(h, 1, 0)
    for h in (0, 1):
        wait(xpart(h, 2, 0, 0), ag_recv.at[h, 2])
        wait(xpart(h, 2, 0, 1), ag_recv.at[h, 3])
        to_b(h, 2)
        to_sib(h, 2, 0)
    for e in (0, 3, 1, 2):
        for h in (0, 1):
            wait(xpart(h, e, 3), ag_recv.at[h, 4 + e])
            forward(h, e, 3, 0, to_ab(h, 0, 1), 12 + e)
            wait(xpart(h, e, 1), ag_recv.at[h, 8 + e])
            forward(h, e, 1, 1, to_ab(h, 0, 3), 16 + e)
            to_sib(h, e, 3)
            to_sib(h, e, 1)
    for e in (0, 3, 1, 2):
        for h in (0, 1):
            wait(xpart(h, e, 2, 0), ag_recv.at[h, 12 + e])
            wait(xpart(h, e, 2, 1), ag_recv.at[h, 16 + e])
            to_sib(h, e, 2)
    for h in (0, 1):
        for da in range(4):
            for db in range(4):
                wait(xpart(h, da, db, None, 1), ag_recv.at[h, 20 + 4 * da + db])
    own_copy.wait()
    tile_copy.wait()
    weight_copy.wait()
    cot_copy.wait()

    acc[...] = jnp.zeros_like(acc)

    def forward_pair(q, carry):
        a = jnp.concatenate([av[table[F_IDX + 2 * q]], av[table[F_IDX + 2 * q + 1]]], axis=1)
        b = jnp.concatenate([xg[table[F_OTH + 2 * q]], xg[table[F_OTH + 2 * q + 1]]], axis=0)
        keep = table[F_KEEP + q].astype(F32)
        total = acc[...] * keep + jnp.dot(a, b, preferred_element_type=F32)
        acc[...] = total
        fout[q] = total.astype(BF)
        return carry

    lax.fori_loop(0, FPAIRS, forward_pair, 0, unroll=4)

    ROWS = TILE // Q

    def hops(d, q):
        return 8 if (d == 0) == (q % 2 == 0) else 7

    def zto(d):
        return dev(dz=1 if d == 0 else -1)

    def zrow(d, q, m):
        dist = hops(d, q) - m
        return (z + dist) % NZ if d == 0 else (z - dist + NZ) % NZ

    def sum_hop(m, first, final):
        for q in range(Q):
            part = pl.ds(q * ROWS, ROWS)
            for d in (0, 1):
                if final and hops(d, q) == 7:
                    continue
                term = fout[table[F_LAST + zrow(d, q, m)], part, :]
                if not first:
                    wait(zr.at[d, m - 1, part], zs_recv.at[d, m - 1, q])
                    term = (term.astype(F32) + zr[d, m - 1, part, :].astype(F32)).astype(BF)
                zs[d, m, part, :] = term
                send(zs.at[d, m, part], zr.at[d, m, part], zs_send, zs_recv.at[d, m, q], zto(d))

    sum_hop(0, True, False)

    def sum_step(m, carry):
        sum_hop(m, False, False)
        return carry

    lax.fori_loop(1, 7, sum_step, 0)
    sum_hop(7, False, True)
    totals = []
    for q in range(Q):
        part = pl.ds(q * ROWS, ROWS)
        total = fout[table[F_LAST + z], part, :].astype(F32)
        for d in (0, 1):
            m = hops(d, q) - 1
            wait(zr.at[d, m, part], zs_recv.at[d, m, q])
            total = total + zr[d, m, part, :].astype(F32)
        totals.append(total.astype(BF))
    agg = jnp.concatenate(totals, axis=0)

    w = wv[...]
    pre = jnp.dot(agg, w, preferred_element_type=F32)
    sig = jax.nn.sigmoid(pre)
    grad_pre = (cv[...].astype(F32) * sig * (1.0 + pre * (1.0 - sig))).astype(BF)
    gt[z] = lax.dot_general(w, grad_pre, (((1,), (1,)), ((), ())), preferred_element_type=F32).astype(BF)

    FR = F // Q

    def zpiece(d, m):
        return (z - m + NZ) % NZ if d == 0 else (z + m) % NZ

    def gather_hop(m):
        for q in range(Q):
            part = pl.ds(q * FR, FR)
            for d in (0, 1):
                ref = gt.at[zpiece(d, m), part]
                if m > 0:
                    wait(ref, zg_recv.at[d, m - 1, q])
                if m < hops(d, q):
                    send(ref, ref, zg_send, zg_recv.at[d, m, q], zto(d))

    gather_hop(0)
    hv[...] = (pre * sig).astype(BF)
    hidden_copy = pltpu.make_async_copy(hv, hidden_o, out_sem.at[0])
    hidden_copy.start()
    lw[...] = lax.dot_general(agg, grad_pre, (((0,), (0,)), ((), ())), preferred_element_type=F32)
    for k in range(4):
        w1s[k] = lw[pl.ds(64 * k, 64), :].astype(BF)

    def w_stage1():
        for k in (1, 2, 3):
            send(w1s.at[(y + k) % NY], w1r.at[k - 1], w_send.at[0], w_recv.at[0], dev(dy=k))

    def w_stage2():
        wait(w1r, w_recv.at[0])
        total = lw[pl.ds(pl.multiple_of(64 * y, 64), 64), :]
        for k in range(3):
            total = total + w1r[k].astype(F32)
        for k in range(4):
            w2s[k] = total[16 * k : 16 * k + 16, :].astype(BF)
        for k in (1, 2, 3):
            send(w2s.at[(x + k) % NX], w2r.at[k - 1], w_send.at[1], w_recv.at[1], dev(dx=k))

    def w_stage3():
        wait(w2r, w_recv.at[1])
        total = w2s[x].astype(F32)
        for k in range(3):
            total = total + w2r[k].astype(F32)
        w3s[0] = total[:, :128].astype(BF)
        w3s[1] = total[:, 128:].astype(BF)
        send(w3s.at[1 - core], w3r, w_send.at[2], w_recv.at[2], dev(flip=1))

    def w_stage4():
        wait(w3r, w_recv.at[2])
        w4[zi] = (w3s[core].astype(F32) + w3r[...].astype(F32)).astype(BF)
        for k in (1, 2, 3):
            send(w4.at[zi], w4.at[zi], w_send.at[3], w_recv.at[3], dev(zz=zq * 4 + (zi + k) % 4))

    def sum4(ref):
        total = ref[0].astype(F32)
        for k in (1, 2, 3):
            total = total + ref[k].astype(F32)
        return total.astype(BF)

    def w_stage5():
        wait(w4.at[pl.ds(0, 3)], w_recv.at[3])
        w5[zq] = sum4(w4)
        for k in (1, 2, 3):
            send(w5.at[zq], w5.at[zq], w_send.at[4], w_recv.at[4], dev(dz=4 * k))

    def w_stage6():
        wait(w5.at[pl.ds(0, 3)], w_recv.at[4])
        w6[core] = sum4(w5)
        send(w6.at[core], w6.at[core], w_send.at[5], w_recv.at[5], dev(flip=1))

    def w_stage7():
        wait(w6.at[0], w_recv.at[5])
        w7[x] = w6[...]
        for k in (1, 2, 3):
            send(w7.at[x], w7.at[x], w_send.at[6], w_recv.at[6], dev(dx=k))

    def w_stage8():
        wait(w7.at[pl.ds(0, 3)], w_recv.at[6])
        w8[y] = w7[...]
        for k in (1, 2, 3):
            send(w8.at[y], w8.at[y], w_send.at[7], w_recv.at[7], dev(dy=k))

    def w_stage9():
        wait(w8.at[pl.ds(0, 3)], w_recv.at[7])
        for i in range(4):
            for j in range(4):
                for k in range(2):
                    gwv[pl.ds(64 * i + 16 * j, 16), pl.ds(128 * k, 128)] = w8[i, j, k].astype(F32)
        gw_copy = pltpu.make_async_copy(gwv, gw_o, out_sem.at[1])
        gw_copy.start()
        return gw_copy

    w_stage1()
    for m in range(1, 9):
        for q in range(Q):
            part = pl.ds(q * FR, FR)
            for d in (0, 1):
                if m > hops(d, q):
                    continue
                ref = gt.at[zpiece(d, m), part]
                wait(ref, zg_recv.at[d, m - 1, q])
                if m < hops(d, q):
                    send(ref, ref, zg_send, zg_recv.at[d, m, q], zto(d))
        if m == 3:
            w_stage2()
        if m == 5:
            w_stage3()
        if m == 7:
            w_stage4()

    w_stage5()

    def backward_pair(q, carry):
        a = jnp.concatenate([gt[table[B_OTH + 2 * q]], gt[table[B_OTH + 2 * q + 1]]], axis=1)
        b = jnp.concatenate([av[table[B_IDX + 2 * q]], av[table[B_IDX + 2 * q + 1]]], axis=0)
        keep = table[B_KEEP + q].astype(F32)
        total = gfv[...] * keep + jnp.dot(a, b, preferred_element_type=F32)
        gfv[...] = total
        bout[q] = total.astype(BF)
        return carry

    gfv[...] = jnp.zeros_like(gfv)
    lax.fori_loop(0, BPAIRS // 2, backward_pair, 0, unroll=4)
    w_stage6()
    lax.fori_loop(BPAIRS // 2, BPAIRS, backward_pair, 0, unroll=4)
    w_stage7()

    def term(h, g, e, flip=0):
        dx, dy = (e, g) if h == 0 else (g, e)
        c = 8 * ((y + dy) % NY) + 2 * ((x + dx) % NX) + (core + flip) % 2
        return bout[table[B_LAST + c], pl.ds(128 * h, 128), :]

    def to_h(h, da, db):
        return dev(dx=db, dy=da) if h == 0 else dev(dx=da, dy=db)

    for g in range(4):
        for h in (0, 1):
            for e in range(4):
                sib_s[h, g, e] = term(h, REL[g], REL[e], 1)
            send(sib_s.at[h, g], sib_r.at[h, g], sb_send, sb_recv.at[h, g], dev(flip=1))

    def both(h, g, e):
        return term(h, REL[g], REL[e]).astype(F32) + sib_r[h, g, e].astype(F32)

    for h in (0, 1):
        wait(sib_r.at[h, 0], sb_recv.at[h, 0])
        for e in range(4):
            total = both(h, 0, e).astype(BF)
            d2s[h, 0, e] = total[:64]
            d2s[h, 1, e] = total[64:]
        send(d2s.at[h, 0], d2r.at[h, 0], rp_send.at[0], rp_recv.at[h, 0], to_h(h, 1, 0))
        send(d2s.at[h, 1], d2r.at[h, 1], rp_send.at[0], rp_recv.at[h, 1], to_h(h, 3, 0))
    for h in (0, 1):
        for d in (0, 1):
            wait(sib_r.at[h, 1 + d], sb_recv.at[h, 1 + d])
            wait(d2r.at[h, d], rp_recv.at[h, d])
            for e in range(4):
                total = both(h, 1 + d, e)
                got = d2r[h, d, e].astype(F32)
                if d == 0:
                    total = jnp.concatenate([total[:64] + got, total[64:]], axis=0)
                else:
                    total = jnp.concatenate([total[:64], total[64:] + got], axis=0)
                d1s[h, d, e] = total.astype(BF)
            send(d1s.at[h, d], d1r.at[h, d], rp_send.at[1], rp_recv.at[h, 2 + d], to_h(h, 1 + 2 * d, 0))
    w_stage8()
    for h in (0, 1):
        wait(sib_r.at[h, 3], sb_recv.at[h, 3])
        for d in (0, 1):
            wait(d1r.at[h, d], rp_recv.at[h, 2 + d])
        for e in range(4):
            vv[h, e] = both(h, 3, e) + d1r[h, 0, e].astype(F32) + d1r[h, 1, e].astype(F32)
            if e == 0:
                total = vv[h, 0].astype(BF)
                e2s[h, 0] = total[:64]
                e2s[h, 1] = total[64:]
                send(e2s.at[h, 0], e2r.at[h, 0], rp_send.at[2], rp_recv.at[h, 4], to_h(h, 0, 1))
                send(e2s.at[h, 1], e2r.at[h, 1], rp_send.at[2], rp_recv.at[h, 5], to_h(h, 0, 3))
    for h in (0, 1):
        for d in (0, 1):
            wait(e2r.at[h, d], rp_recv.at[h, 4 + d])
            total = vv[h, 1 + d]
            got = e2r[h, d].astype(F32)
            if d == 0:
                total = jnp.concatenate([total[:64] + got, total[64:]], axis=0)
            else:
                total = jnp.concatenate([total[:64], total[64:] + got], axis=0)
            e1s[h, d] = total.astype(BF)
            send(e1s.at[h, d], e1r.at[h, d], rp_send.at[3], rp_recv.at[h, 6 + d], to_h(h, 0, 1 + 2 * d))
    gw_copy = w_stage9()
    for h in (0, 1):
        for d in (0, 1):
            wait(e1r.at[h, d], rp_recv.at[h, 6 + d])
        gft[pl.ds(128 * h, 128), :] = vv[h, 3] + e1r[h, 0].astype(F32) + e1r[h, 1].astype(F32)
    hv2 = xg.at[NCOLS]
    hv2[...] = jnp.transpose(gft[...]).astype(BF)
    gf_copy = pltpu.make_async_copy(hv2, gf_o, out_sem.at[2])
    gf_copy.start()

    hidden_copy.wait()
    gw_copy.wait()
    gf_copy.wait()
    wait(xg.at[pl.ds(0, NCOLS - 1)], ag_send)
    wait(xg.at[pl.ds(0, NZ - 1)], zs_send)
    wait(xg.at[pl.ds(0, NZ - 1)], zg_send)
    wait(sib_s, sb_send)
    wait(d2s, rp_send.at[0])
    wait(d1s, rp_send.at[1])
    wait(e2s, rp_send.at[2])
    wait(e1s, rp_send.at[3])
    wait(w1r, w_send.at[0])
    wait(w2r, w_send.at[1])
    wait(w3r, w_send.at[2])
    wait(w4.at[pl.ds(0, 3)], w_send.at[3])
    wait(w5.at[pl.ds(0, 3)], w_send.at[4])
    wait(w6.at[0], w_send.at[5])
    wait(w7.at[pl.ds(0, 3)], w_send.at[6])
    wait(w8.at[pl.ds(0, 3)], w_send.at[7])


def per_device(feats, tile_values, tile_rows, tile_cols, tile_count, weight, cotangent):
    tiles = tile_values.reshape(tile_values.shape[3:])
    tile_row, tile_col = tile_rows.reshape(-1), tile_cols.reshape(-1)
    live = lax.iota(jnp.int32, SLOTS) < tile_count.reshape(())
    table = jnp.concatenate(
        schedule(tile_row, tile_col, live, NROWS, NCOLS) + schedule(tile_col, tile_row, live, NCOLS, NZ)
    )
    vm, dma = pltpu.VMEM, pltpu.SemaphoreType.DMA
    scratch = [
        vm((SLOTS, TILE, TILE), BF),
        vm((NCOLS + 1, TILE, F), BF),
        vm((FPAIRS + 1, TILE, F), BF),
        vm((TILE, F), F32),
        vm((F, F), BF),
        vm((TILE, F), BF),
        vm((2, 8, TILE, F), BF),
        vm((2, 8, TILE, F), BF),
        vm((NZ + 1, F, TILE), BF),
        vm((BPAIRS + 1, F, TILE), BF),
        vm((2, 4, 4, 128, TILE), BF),
        vm((2, 4, 4, 128, TILE), BF),
        vm((2, 2, 4, 64, TILE), BF),
        vm((2, 2, 4, 64, TILE), BF),
        vm((2, 2, 4, 128, TILE), BF),
        vm((2, 2, 4, 128, TILE), BF),
        vm((2, 4, 128, TILE), F32),
        vm((2, 2, 64, TILE), BF),
        vm((2, 2, 64, TILE), BF),
        vm((2, 2, 128, TILE), BF),
        vm((2, 2, 128, TILE), BF),
        vm((F, TILE), F32),
        vm((F, TILE), F32),
        vm((TILE, F), BF),
        vm((4, 64, F), BF),
        vm((3, 64, F), BF),
        vm((4, 16, F), BF),
        vm((3, 16, F), BF),
        vm((2, 16, 128), BF),
        vm((16, 128), BF),
        vm((4, 16, 128), BF),
        vm((4, 16, 128), BF),
        vm((2, 16, 128), BF),
        vm((4, 2, 16, 128), BF),
        vm((4, 4, 2, 16, 128), BF),
        vm((F, F), F32),
        vm((F, F), F32),
        dma((4,)),
        dma,
        dma((2, 36)),
        dma,
        dma((2, 8, Q)),
        dma,
        dma((2, 8, Q)),
        dma,
        dma((2, 4)),
        dma((4,)),
        dma((2, 8)),
        dma((8,)),
        dma((8,)),
        dma((3,)),
    ]
    any_spec = pl.BlockSpec(memory_space=pl.ANY)
    hidden, grad_feats, grad_weight = pl.pallas_call(
        kernel,
        out_shape=(
            jax.ShapeDtypeStruct((TILE, F), BF),
            jax.ShapeDtypeStruct((TILE, F), BF),
            jax.ShapeDtypeStruct((F, F), F32),
        ),
        in_specs=[pl.BlockSpec(memory_space=pltpu.SMEM)] + [any_spec] * 4,
        out_specs=(any_spec,) * 3,
        scratch_shapes=scratch,
        compiler_params=pltpu.CompilerParams(
            collective_id=0, has_side_effects=True, vmem_limit_bytes=40 * 1024 * 1024
        ),
        cost_estimate=pl.CostEstimate(flops=2_000_000_000, bytes_accessed=4_000_000, transcendentals=32768),
    )(table, feats, tiles, weight, cotangent)
    nodes = TILE * NX * NY * NZ * 2
    return hidden, grad_feats, grad_weight * nodes ** (-0.5)


def solution(mesh):
    return jax.shard_map(
        per_device,
        mesh=mesh,
        in_specs=(
            P(("row", "col", "depth"), None),
            P("row", "col", "depth", None, None, None),
            P("row", "col", "depth", None),
            P("row", "col", "depth", None),
            P("row", "col", "depth"),
            P(),
            P(("row", "col", "depth"), None),
        ),
        out_specs=(P(("row", "col", "depth"), None), P(("row", "col", "depth"), None), P()),
        check_vma=False,
    )
```

```python
import jax
import jax.numpy as jnp
from jax import lax
from jax.experimental import pallas as pl
from jax.experimental.pallas import tpu as pltpu
from jax.sharding import PartitionSpec as P

MESH = pl.DeviceIdType.MESH
BF, F32 = jnp.bfloat16, jnp.float32

NX, NY, NZ = 4, 4, 16
TILE, F, SLOTS = 128, 256, 96
NROWS, NCOLS = NZ, NX * NY * 2
FPOS, BPOS = SLOTS + NROWS, SLOTS + NCOLS
FPAIRS, BPAIRS = FPOS // 2, BPOS // 2
Q = 2
REL = (2, 1, 3, 0)

F_IDX, F_OTH, F_KEEP, F_LAST, B_IDX, B_OTH, B_KEEP, B_LAST = range(8)


def schedule(keys, others, count, zero, none):
    full = (128, 128)
    lane, sub = lax.broadcasted_iota(jnp.int32, full, 1), lax.broadcasted_iota(jnp.int32, full, 0)

    def down(ref):
        return jnp.transpose(jnp.broadcast_to(ref, full))

    key = jnp.broadcast_to(keys, full)
    key_down = jnp.transpose(key)
    live = lane < count
    same = (key == key_down) & (sub < lane) & (sub < count)
    rank = jnp.sum(jnp.where(same, 1, 0), axis=0, keepdims=True)
    hot = (key == sub) & live
    number = jnp.sum(jnp.where(hot, 1, 0), axis=1, keepdims=True)
    padded = jnp.broadcast_to(lax.shift_left(lax.shift_right_logical(number + 1, 1), 1), full)
    place = rank + jnp.sum(jnp.where(sub < key, padded, 0), axis=0, keepdims=True)
    place = jnp.where(live, jnp.broadcast_to(place, full), 1000)
    at = jnp.transpose(place) == lane
    slot = jnp.sum(jnp.where(at, sub, 0), axis=0, keepdims=True)
    other = jnp.sum(jnp.where(at, down(others) - zero, 0), axis=0, keepdims=True) + zero
    keep = 1 - jnp.sum(jnp.where(at & (down(rank) == 0), 1, 0), axis=0, keepdims=True)
    last = jnp.max(jnp.where(hot, lax.shift_right_logical(place, 1), -1), axis=1, keepdims=True)
    last = down_first(jnp.where(number > 0, last, none), full)
    return [slot, other, keep, last]


def down_first(column, full):
    return jnp.transpose(jnp.broadcast_to(column, full))[:1]


def wait(ref, sem):
    pltpu.make_async_copy(ref, ref, sem).wait()


def kernel(
    counts, rows_i, cols_i, feats, tiles, weight, cot, hidden_o, gf_o, gw_o,
    rows_v, cols_v, pad, table_v, table, av, xg, fout, acc, wv, cv, zs, zr, gt, bout, sib_s, sib_r,
    ps, pr, qs, qr, vv, gft, gfv, hv,
    w1s, w1r, w2s, w2r, w3s, w3r, w4, w5, w6, w7, w8, lw, gwv,
    loc, ag_send, ag_recv, zs_send, zs_recv, zg_send, zg_recv,
    sb_send, sb_recv, rp_send, rp_recv, w_send, w_recv, out_sem,
):
    row, z, depth = lax.axis_index("row"), lax.axis_index("col"), lax.axis_index("depth")
    y, x, core = row // 2, (row % 2) * 2 + depth // 2, depth % 2

    def dev(dx=0, dy=0, dz=0, flip=0, zz=None):
        nx, ny = (x + dx) % NX, (y + dy) % NY
        nz = (z + dz + NZ) % NZ if zz is None else zz
        nc = (core + flip) % 2
        return {"row": ny * 2 + nx // 2, "col": nz, "depth": (nx % 2) * 2 + nc}

    def send(src, dst, ssem, rsem, to):
        pltpu.make_async_remote_copy(
            src_ref=src, dst_ref=dst, send_sem=ssem, recv_sem=rsem, device_id=to, device_id_type=MESH
        ).start()

    zi, zq = z % 4, z // 4
    partners = [dev(flip=1), dev(dz=1), dev(dz=-1), dev(dz=4), dev(dz=-4)]
    for k in (1, 2, 3):
        partners += [dev(dx=k), dev(dy=k), dev(zz=zq * 4 + (zi + k) % 4)]
    barrier = pltpu.get_barrier_semaphore()
    for to in partners:
        pl.semaphore_signal(barrier, inc=1, device_id=to, device_id_type=MESH)

    mine = 8 * y + 2 * x + core
    local = []
    for k, (src, dst) in enumerate(
        [(rows_i, rows_v), (cols_i, cols_v), (feats, xg.at[mine]), (tiles.at[0, 0, 0], av), (weight, wv), (cot, cv)]
    ):
        local.append(pltpu.make_async_copy(src, dst, loc.at[k]))
        local[k].start()
    pl.semaphore_wait(barrier, len(partners))

    def to_ab(h, da, db):
        return dev(dx=da, dy=db) if h == 0 else dev(dx=db, dy=da)

    def piece(h, da, db, flip=0):
        dx, dy = (da, db) if h == 0 else (db, da)
        return 8 * ((y + dy) % NY) + 2 * ((x + dx) % NX) + (core + flip) % 2

    def xpart(h, da, db, flip=0):
        return xg.at[piece(h, da, db, flip), pl.ds(64 * h, 64)]

    def forward(h, da, db, to, k, own):
        src = feats.at[pl.ds(64 * h, 64)] if own else xpart(h, da, db)
        send(src, xpart(h, da, db), ag_send, ag_recv.at[h, k], to)

    def to_a(h, k):
        forward(h, 0, 0, to_ab(h, k, 0), k - 1, True)

    def to_b(h, e, k, own=False):
        forward(h, e, 0, to_ab(h, 0, k), 3 + 3 * e + k - 1, own)

    def to_sib(h, da, db, own=False):
        forward(h, da, db, dev(flip=1), 15 + 4 * da + db, own)

    for k in (2, 1, 3):
        for h in (0, 1):
            to_a(h, k)
    for k in (2, 1, 3):
        for h in (0, 1):
            to_b(h, 0, k, True)
    for h in (0, 1):
        to_sib(h, 0, 0, True)

    xg[NCOLS] = jnp.zeros((TILE, F), BF)
    gt[NZ] = jnp.zeros((F, TILE), BF)
    fout[FPAIRS] = jnp.zeros((TILE, F), BF)
    bout[BPAIRS] = jnp.zeros((F, TILE), BF)
    acc[...] = jnp.zeros_like(acc)
    pad[...] = jnp.zeros_like(pad)
    local[0].wait()
    local[1].wait()
    pad[0:1, 0:SLOTS] = rows_v[0, 0]
    pad[1:2, 0:SLOTS] = cols_v[0, 0]
    live_count = counts[0, 0, 0]
    by_row = schedule(pad[0:1], pad[1:2], live_count, NCOLS, FPAIRS)
    by_col = schedule(pad[1:2], pad[0:1], live_count, NZ, BPAIRS)
    for k, line in enumerate(by_row + by_col):
        table_v[k : k + 1, :] = line
    table_copy = pltpu.make_async_copy(table_v, table, loc.at[6])
    table_copy.start()

    for k in (1, 3, 2):
        for h in (0, 1):
            wait(xpart(h, 4 - k, 0), ag_recv.at[h, k - 1])
            for kb in (2, 1, 3):
                to_b(h, 4 - k, kb)
            to_sib(h, 4 - k, 0)
    for e in (0, 3, 1, 2):
        for k in (1, 3, 2):
            for h in (0, 1):
                wait(xpart(h, e, 4 - k), ag_recv.at[h, 3 + 3 * e + k - 1])
                to_sib(h, e, 4 - k)
    for h in (0, 1):
        for da in range(4):
            for db in range(4):
                wait(xpart(h, da, db, 1), ag_recv.at[h, 15 + 4 * da + db])
    for copy in local[2:]:
        copy.wait()
    table_copy.wait()

    def forward_pair(q, carry):
        a = jnp.concatenate([av[table[F_IDX, 2 * q]], av[table[F_IDX, 2 * q + 1]]], axis=1)
        b = jnp.concatenate([xg[table[F_OTH, 2 * q]], xg[table[F_OTH, 2 * q + 1]]], axis=0)
        keep = table[F_KEEP, 2 * q].astype(F32)
        total = acc[...] * keep + jnp.dot(a, b, preferred_element_type=F32)
        acc[...] = total
        fout[q] = total.astype(BF)
        return carry

    lax.fori_loop(0, FPAIRS, forward_pair, 0, unroll=4)

    ROWS = TILE // Q

    def farthest(d, q):
        return 8 if (d == 0) == (q % 2 == 0) else 7

    def zat(d, dist):
        return (z + dist) % NZ if d == 0 else (z - dist + NZ) % NZ

    def zto(d, step=1):
        return dev(dz=step if d == 0 else -step)

    def sum_hop(dist):
        for q in range(Q):
            part = pl.ds(q * ROWS, ROWS)
            for d in (0, 1):
                far = farthest(d, q)
                if dist > far:
                    continue
                term = fout[table[F_LAST, zat(d, dist)], part, :]
                if dist not in (far, 3):
                    wait(zr.at[d, dist, part], zs_recv.at[d, dist, q])
                    term = (term.astype(F32) + zr[d, dist, part, :].astype(F32)).astype(BF)
                zs[d, dist - 1, part, :] = term
                send(
                    zs.at[d, dist - 1, part], zr.at[d, 0 if dist == 4 else (8 if dist == 1 else dist - 1), part], zs_send,
                    zs_recv.at[d, 8 if dist == 4 else dist - 1, q], zto(d, 4 if dist == 4 else 1),
                )

    for dist in (8, 7, 3, 6, 2, 5, 1, 4):
        sum_hop(dist)
    totals = []
    for q in range(Q):
        part = pl.ds(q * ROWS, ROWS)
        total = fout[table[F_LAST, z], part, :].astype(F32)
        for d in (0, 1):
            for slot, sem in ((8, 0), (0, 8)):
                wait(zr.at[d, slot, part], zs_recv.at[d, sem, q])
                total = total + zr[d, slot, part, :].astype(F32)
        totals.append(total.astype(BF))
    agg = jnp.concatenate(totals, axis=0)

    w = wv[...]
    pre = jnp.dot(agg, w, preferred_element_type=F32)
    sig = jax.nn.sigmoid(pre)
    grad_pre = (cv[...].astype(F32) * sig * (1.0 + pre * (1.0 - sig))).astype(BF)
    gt[z] = lax.dot_general(w, grad_pre, (((1,), (1,)), ((), ())), preferred_element_type=F32).astype(BF)

    FR = F // Q

    def gather_from(dist):
        for q in range(Q):
            part = pl.ds(q * FR, FR)
            for d in (0, 1):
                far = farthest(d, q)
                if dist > far:
                    continue
                ref = gt.at[zat(1 - d, dist), part]
                if dist > 0:
                    wait(ref, zg_recv.at[d, dist, q])
                if dist == 0:
                    send(ref, ref, zg_send, zg_recv.at[d, 4, q], zto(d, 4))
                if dist != 3 and dist < far:
                    send(ref, ref, zg_send, zg_recv.at[d, dist + 1, q], zto(d))

    gather_from(0)
    hv[...] = (pre * sig).astype(BF)
    hidden_copy = pltpu.make_async_copy(hv, hidden_o, out_sem.at[0])
    hidden_copy.start()
    lw[...] = lax.dot_general(agg, grad_pre, (((0,), (0,)), ((), ())), preferred_element_type=F32)
    for k in range(4):
        w1s[k] = lw[pl.ds(64 * k, 64), :].astype(BF)

    def w_stage1():
        for k in (1, 2, 3):
            send(w1s.at[(y + k) % NY], w1r.at[k - 1], w_send.at[0], w_recv.at[0], dev(dy=k))

    def w_stage2():
        wait(w1r, w_recv.at[0])
        total = lw[pl.ds(pl.multiple_of(64 * y, 64), 64), :]
        for k in range(3):
            total = total + w1r[k].astype(F32)
        for k in range(4):
            w2s[k] = total[16 * k : 16 * k + 16, :].astype(BF)
        for k in (1, 2, 3):
            send(w2s.at[(x + k) % NX], w2r.at[k - 1], w_send.at[1], w_recv.at[1], dev(dx=k))

    def w_stage3():
        wait(w2r, w_recv.at[1])
        total = w2s[x].astype(F32)
        for k in range(3):
            total = total + w2r[k].astype(F32)
        w3s[0] = total[:, :128].astype(BF)
        w3s[1] = total[:, 128:].astype(BF)
        send(w3s.at[1 - core], w3r, w_send.at[2], w_recv.at[2], dev(flip=1))

    def w_stage4():
        wait(w3r, w_recv.at[2])
        w4[zi] = (w3s[core].astype(F32) + w3r[...].astype(F32)).astype(BF)
        for k in (1, 2, 3):
            send(w4.at[zi], w4.at[zi], w_send.at[3], w_recv.at[3], dev(zz=zq * 4 + (zi + k) % 4))

    def sum4(ref):
        total = ref[0].astype(F32)
        for k in (1, 2, 3):
            total = total + ref[k].astype(F32)
        return total.astype(BF)

    def w_stage5():
        wait(w4.at[pl.ds(0, 3)], w_recv.at[3])
        w5[zq] = sum4(w4)
        for d in (0, 1):
            send(w5.at[zq], w5.at[zq], w_send.at[4], w_recv.at[4 + d], zto(d, 4))

    def w_stage6():
        for d in (0, 1):
            wait(w5.at[(zq + 3 + 2 * d) % 4], w_recv.at[4 + d])
        send(w5.at[(zq + 3) % 4], w5.at[(zq + 3) % 4], w_send.at[5], w_recv.at[6], dev(dz=4))

    def w_stage7():
        wait(w5.at[(zq + 2) % 4], w_recv.at[6])
        w6[core] = sum4(w5)
        send(w6.at[core], w6.at[core], w_send.at[6], w_recv.at[7], dev(flip=1))

    def w_stage8():
        wait(w6.at[1 - core], w_recv.at[7])
        w7[x] = w6[...]
        for k in (1, 2, 3):
            send(w7.at[x], w7.at[x], w_send.at[7], w_recv.at[8], dev(dx=k))

    def w_stage9():
        wait(w7.at[pl.ds(0, 3)], w_recv.at[8])
        w8[y] = w7[...]
        for k in (1, 2, 3):
            send(w8.at[y], w8.at[y], w_send.at[8], w_recv.at[9], dev(dy=k))

    def w_stage10():
        wait(w8.at[pl.ds(0, 3)], w_recv.at[9])
        scale = (TILE * NX * NY * NZ * 2) ** -0.5
        for i in range(4):
            for j in range(4):
                for k in range(2):
                    gwv[pl.ds(64 * i + 16 * j, 16), pl.ds(128 * k, 128)] = w8[i, j, k].astype(F32) * scale
        gw_copy = pltpu.make_async_copy(gwv, gw_o, out_sem.at[1])
        gw_copy.start()
        return gw_copy

    w_stage1()
    gather_from(1)
    gather_from(2)
    w_stage2()
    gather_from(4)
    gather_from(5)
    w_stage3()
    gather_from(6)
    w_stage4()
    gather_from(7)
    gather_from(3)
    gather_from(8)
    w_stage5()

    def products(h):
        half = pl.ds(128 * h, 128)

        def backward_pair(q, carry):
            a = jnp.concatenate([gt[table[B_OTH, 2 * q], half, :], gt[table[B_OTH, 2 * q + 1], half, :]], axis=1)
            b = jnp.concatenate([av[table[B_IDX, 2 * q]], av[table[B_IDX, 2 * q + 1]]], axis=0)
            keep = table[B_KEEP, 2 * q].astype(F32)
            total = gfv[half, :] * keep + jnp.dot(a, b, preferred_element_type=F32)
            gfv[half, :] = total
            bout[q, half, :] = total.astype(BF)
            return carry

        gfv[half, :] = jnp.zeros((128, TILE), F32)
        lax.fori_loop(0, BPAIRS, backward_pair, 0, unroll=4)

    def term(h, g, e, flip=0):
        dx, dy = (e, g) if h == 0 else (g, e)
        c = 8 * ((y + dy) % NY) + 2 * ((x + dx) % NX) + (core + flip) % 2
        return bout[table[B_LAST, c], pl.ds(128 * h, 128), :]

    def to_h(h, da, db):
        return dev(dx=db, dy=da) if h == 0 else dev(dx=da, dy=db)

    def to_sibling(h):
        for g in range(4):
            for e in range(4):
                sib_s[h, g, e] = term(h, REL[g], REL[e], 1)
            send(sib_s.at[h, g], sib_r.at[h, g], sb_send, sb_recv.at[h, g], dev(flip=1))

    def both(h, g, e):
        return term(h, REL[g], REL[e]).astype(F32) + sib_r[h, g, e].astype(F32)

    def first_axis(h):
        for g in range(3):
            wait(sib_r.at[h, g], sb_recv.at[h, g])
            for e in range(4):
                ps[h, g, e] = both(h, g, e).astype(BF)
            send(ps.at[h, g], pr.at[h, g], rp_send.at[0], rp_recv.at[h, g], to_h(h, REL[g], 0))

    def second_axis(h):
        wait(sib_r.at[h, 3], sb_recv.at[h, 3])
        for g in range(3):
            wait(pr.at[h, g], rp_recv.at[h, g])
        for e in range(4):
            total = both(h, 3, e)
            for g in range(3):
                total = total + pr[h, g, e].astype(F32)
            if e < 3:
                qs[h, e] = total.astype(BF)
                send(qs.at[h, e], qr.at[h, e], rp_send.at[1], rp_recv.at[h, 3 + e], to_h(h, 0, REL[e]))
            else:
                vv[h] = total

    products(0)
    to_sibling(0)
    w_stage6()
    products(1)
    to_sibling(1)
    first_axis(0)
    first_axis(1)
    w_stage7()
    second_axis(0)
    w_stage8()
    second_axis(1)
    w_stage9()
    for h in (0, 1):
        total = vv[h]
        for e in range(3):
            wait(qr.at[h, e], rp_recv.at[h, 3 + e])
            total = total + qr[h, e].astype(F32)
        gft[pl.ds(128 * h, 128), :] = total
    hv2 = xg.at[NCOLS]
    hv2[...] = jnp.transpose(gft[...]).astype(BF)
    gf_copy = pltpu.make_async_copy(hv2, gf_o, out_sem.at[2])
    gf_copy.start()
    gw_copy = w_stage10()

    hidden_copy.wait()
    gw_copy.wait()
    gf_copy.wait()
    wait(xg.at[pl.ds(0, NCOLS - 1)], ag_send)
    wait(xg.at[pl.ds(0, NZ - 1)], zs_send)
    wait(xg.at[pl.ds(0, NZ - 1)], zg_send)
    wait(sib_s, sb_send)
    wait(ps, rp_send.at[0])
    wait(qs, rp_send.at[1])
    wait(w1r, w_send.at[0])
    wait(w2r, w_send.at[1])
    wait(w3r, w_send.at[2])
    wait(w4.at[pl.ds(0, 3)], w_send.at[3])
    wait(w5.at[pl.ds(0, 2)], w_send.at[4])
    wait(w5.at[0], w_send.at[5])
    wait(w6.at[0], w_send.at[6])
    wait(w7.at[pl.ds(0, 3)], w_send.at[7])
    wait(w8.at[pl.ds(0, 3)], w_send.at[8])


def per_device(feats, tile_values, tile_rows, tile_cols, tile_count, weight, cotangent):
    vm, dma = pltpu.VMEM, pltpu.SemaphoreType.DMA
    scratch = [
        vm((1, 1, 1, SLOTS), jnp.int32),
        vm((1, 1, 1, SLOTS), jnp.int32),
        vm((8, 128), jnp.int32),
        vm((8, 128), jnp.int32),
        pltpu.SMEM((8, 128), jnp.int32),
        vm((SLOTS, TILE, TILE), BF),
        vm((NCOLS + 1, TILE, F), BF),
        vm((FPAIRS + 1, TILE, F), BF),
        vm((TILE, F), F32),
        vm((F, F), BF),
        vm((TILE, F), BF),
        vm((2, 8, TILE, F), BF),
        vm((2, 9, TILE, F), BF),
        vm((NZ + 1, F, TILE), BF),
        vm((BPAIRS + 1, F, TILE), BF),
        vm((2, 4, 4, 128, TILE), BF),
        vm((2, 4, 4, 128, TILE), BF),
        vm((2, 3, 4, 128, TILE), BF),
        vm((2, 3, 4, 128, TILE), BF),
        vm((2, 3, 128, TILE), BF),
        vm((2, 3, 128, TILE), BF),
        vm((2, 128, TILE), F32),
        vm((F, TILE), F32),
        vm((F, TILE), F32),
        vm((TILE, F), BF),
        vm((4, 64, F), BF),
        vm((3, 64, F), BF),
        vm((4, 16, F), BF),
        vm((3, 16, F), BF),
        vm((2, 16, 128), BF),
        vm((16, 128), BF),
        vm((4, 16, 128), BF),
        vm((4, 16, 128), BF),
        vm((2, 16, 128), BF),
        vm((4, 2, 16, 128), BF),
        vm((4, 4, 2, 16, 128), BF),
        vm((F, F), F32),
        vm((F, F), F32),
        dma((7,)),
        dma,
        dma((2, 31)),
        dma,
        dma((2, 9, Q)),
        dma,
        dma((2, 9, Q)),
        dma,
        dma((2, 4)),
        dma((2,)),
        dma((2, 6)),
        dma((9,)),
        dma((10,)),
        dma((3,)),
    ]
    any_spec = pl.BlockSpec(memory_space=pltpu.HBM)
    hidden, grad_feats, grad_weight = pl.pallas_call(
        kernel,
        out_shape=(
            jax.ShapeDtypeStruct((TILE, F), BF),
            jax.ShapeDtypeStruct((TILE, F), BF),
            jax.ShapeDtypeStruct((F, F), F32),
        ),
        in_specs=[pl.BlockSpec(memory_space=pltpu.SMEM)] + [any_spec] * 6,
        out_specs=(any_spec,) * 3,
        scratch_shapes=scratch,
        compiler_params=pltpu.CompilerParams(
            collective_id=0, has_side_effects=True, vmem_limit_bytes=60 * 1024 * 1024
        ),
        cost_estimate=pl.CostEstimate(flops=2_000_000_000, bytes_accessed=4_000_000, transcendentals=32768),
    )(tile_count, tile_rows, tile_cols, feats, tile_values, weight, cotangent)
    return hidden, grad_feats, grad_weight


def solution(mesh):
    return jax.shard_map(
        per_device,
        mesh=mesh,
        in_specs=(
            P(("row", "col", "depth"), None),
            P("row", "col", "depth", None, None, None),
            P("row", "col", "depth", None),
            P("row", "col", "depth", None),
            P("row", "col", "depth"),
            P(),
            P(("row", "col", "depth"), None),
        ),
        out_specs=(P(("row", "col", "depth"), None), P(("row", "col", "depth"), None), P()),
        check_vma=False,
    )
```

```python
import jax
import jax.numpy as jnp
from jax import lax
from jax.experimental import pallas as pl
from jax.experimental.pallas import tpu as pltpu
from jax.sharding import PartitionSpec as P

MESH = pl.DeviceIdType.MESH
BF, F32 = jnp.bfloat16, jnp.float32

NX, NY, NZ = 4, 4, 16
TILE, F, SLOTS = 128, 256, 96
NROWS, NCOLS = NZ, NX * NY * 2
FPOS, BPOS = SLOTS + NROWS, SLOTS + NCOLS
FPAIRS, BPAIRS = FPOS // 2, BPOS // 2
Q = 2
REL = (2, 1, 3, 0)

F_IDX, F_OTH, F_KEEP, F_LAST, B_IDX, B_OTH, B_KEEP, B_LAST = range(8)


def schedule(keys, others, count, zero, none):
    full = (128, 128)
    lane, sub = lax.broadcasted_iota(jnp.int32, full, 1), lax.broadcasted_iota(jnp.int32, full, 0)

    def down(ref):
        return jnp.transpose(jnp.broadcast_to(ref, full))

    key = jnp.broadcast_to(keys, full)
    key_down = jnp.transpose(key)
    live = lane < count
    same = (key == key_down) & (sub < lane) & (sub < count)
    rank = jnp.sum(jnp.where(same, 1, 0), axis=0, keepdims=True)
    hot = (key == sub) & live
    number = jnp.sum(jnp.where(hot, 1, 0), axis=1, keepdims=True)
    padded = jnp.broadcast_to(lax.shift_left(lax.shift_right_logical(number + 1, 1), 1), full)
    place = rank + jnp.sum(jnp.where(sub < key, padded, 0), axis=0, keepdims=True)
    place = jnp.where(live, jnp.broadcast_to(place, full), 1000)
    at = jnp.transpose(place) == lane
    slot = jnp.sum(jnp.where(at, sub, 0), axis=0, keepdims=True)
    other = jnp.sum(jnp.where(at, down(others) - zero, 0), axis=0, keepdims=True) + zero
    keep = 1 - jnp.sum(jnp.where(at & (down(rank) == 0), 1, 0), axis=0, keepdims=True)
    last = jnp.max(jnp.where(hot, lax.shift_right_logical(place, 1), -1), axis=1, keepdims=True)
    last = down_first(jnp.where(number > 0, last, none), full)
    return [slot, other, keep, last]


def down_first(column, full):
    return jnp.transpose(jnp.broadcast_to(column, full))[:1]


def wait(ref, sem):
    pltpu.make_async_copy(ref, ref, sem).wait()


def kernel(
    counts, rows_i, cols_i, feats, tiles, weight, cot, hidden_o, gf_o, gw_o,
    rows_v, cols_v, pad, table_v, table, av, xg, fout, acc, wv, cv, zs, zr, gt0, gt1, bout, sib_s, sib_r,
    ps, pr, qs, qr, vv, gft, gfv, hv,
    w1s, w1r, w2s, w2r, w3s, w3r, w4, w5, w6, w7, w8, lw, gwv,
    loc, ag_send, ag_recv, zs_send, zs_recv, zg_send, zg_recv,
    sb_send, sb_recv, rp_send, rp_recv, w_send, w_recv, out_sem,
):
    row, z, depth = lax.axis_index("row"), lax.axis_index("col"), lax.axis_index("depth")
    y, x, core = row // 2, (row % 2) * 2 + depth // 2, depth % 2

    def dev(dx=0, dy=0, dz=0, flip=0, zz=None):
        nx, ny = (x + dx) % NX, (y + dy) % NY
        nz = (z + dz + NZ) % NZ if zz is None else zz
        nc = (core + flip) % 2
        return {"row": ny * 2 + nx // 2, "col": nz, "depth": (nx % 2) * 2 + nc}

    def send(src, dst, ssem, rsem, to):
        pltpu.make_async_remote_copy(
            src_ref=src, dst_ref=dst, send_sem=ssem, recv_sem=rsem, device_id=to, device_id_type=MESH
        ).start()

    zi, zq = z % 4, z // 4
    partners = [dev(flip=1)] + [dev(dz=step) for step in (1, -1, 2, -2, 4, -4)]
    for k in (1, 2, 3):
        partners += [dev(dx=k), dev(dy=k), dev(zz=zq * 4 + (zi + k) % 4)]
    barrier = pltpu.get_barrier_semaphore()
    for to in partners:
        pl.semaphore_signal(barrier, inc=1, device_id=to, device_id_type=MESH)

    mine = 8 * y + 2 * x + core
    local = []
    for k, (src, dst) in enumerate(
        [(rows_i, rows_v), (cols_i, cols_v), (feats, xg.at[mine]), (tiles.at[0, 0, 0], av), (weight, wv), (cot, cv)]
    ):
        local.append(pltpu.make_async_copy(src, dst, loc.at[k]))
        local[k].start()
    pl.semaphore_wait(barrier, len(partners))

    def to_ab(h, da, db):
        return dev(dx=da, dy=db) if h == 0 else dev(dx=db, dy=da)

    def piece(h, da, db, flip=0):
        dx, dy = (da, db) if h == 0 else (db, da)
        return 8 * ((y + dy) % NY) + 2 * ((x + dx) % NX) + (core + flip) % 2

    def xpart(h, da, db, flip=0):
        return xg.at[piece(h, da, db, flip), pl.ds(64 * h, 64)]

    def forward(h, da, db, to, k, own):
        src = feats.at[pl.ds(64 * h, 64)] if own else xpart(h, da, db)
        send(src, xpart(h, da, db), ag_send, ag_recv.at[h, k], to)

    def to_a(h, k):
        forward(h, 0, 0, to_ab(h, k, 0), k - 1, True)

    def to_b(h, e, k, own=False):
        forward(h, e, 0, to_ab(h, 0, k), 3 + 3 * e + k - 1, own)

    def to_sib(h, da, db, own=False):
        forward(h, da, db, dev(flip=1), 15 + 4 * da + db, own)

    for k in (2, 1, 3):
        for h in (0, 1):
            to_a(h, k)
    for k in (2, 1, 3):
        for h in (0, 1):
            to_b(h, 0, k, True)
    for h in (0, 1):
        to_sib(h, 0, 0, True)

    xg[NCOLS] = jnp.zeros((TILE, F), BF)
    for part in (gt0, gt1):
        part[NZ] = jnp.zeros((F // 2, TILE), BF)
    fout[FPAIRS] = jnp.zeros((TILE, F), BF)
    bout[BPAIRS] = jnp.zeros((F, TILE), BF)
    acc[...] = jnp.zeros_like(acc)
    pad[...] = jnp.zeros_like(pad)
    local[0].wait()
    local[1].wait()
    pad[0:1, 0:SLOTS] = rows_v[0, 0]
    pad[1:2, 0:SLOTS] = cols_v[0, 0]
    live_count = jnp.broadcast_to(counts[0], (128, 128))
    by_row = schedule(pad[0:1], pad[1:2], live_count, NCOLS, FPAIRS)
    by_col = schedule(pad[1:2], pad[0:1], live_count, NZ, BPAIRS)
    for k, line in enumerate(by_row + by_col):
        table_v[k : k + 1, :] = line
    table_copy = pltpu.make_async_copy(table_v, table, loc.at[6])
    table_copy.start()

    for k in (1, 3, 2):
        for h in (0, 1):
            wait(xpart(h, 4 - k, 0), ag_recv.at[h, k - 1])
            for kb in (2, 1, 3):
                to_b(h, 4 - k, kb)
            to_sib(h, 4 - k, 0)
    for e in (0, 3, 1, 2):
        for k in (1, 3, 2):
            for h in (0, 1):
                wait(xpart(h, e, 4 - k), ag_recv.at[h, 3 + 3 * e + k - 1])
                to_sib(h, e, 4 - k)
    for h in (0, 1):
        for da in range(4):
            for db in range(4):
                wait(xpart(h, da, db, 1), ag_recv.at[h, 15 + 4 * da + db])
    for copy in local[2:]:
        copy.wait()
    table_copy.wait()

    def forward_pair(q, carry):
        a = jnp.concatenate([av[table[F_IDX, 2 * q]], av[table[F_IDX, 2 * q + 1]]], axis=1)
        b = jnp.concatenate([xg[table[F_OTH, 2 * q]], xg[table[F_OTH, 2 * q + 1]]], axis=0)
        keep = table[F_KEEP, 2 * q].astype(F32)
        total = acc[...] * keep + jnp.dot(a, b, preferred_element_type=F32)
        acc[...] = total
        fout[q] = total.astype(BF)
        return carry

    lax.fori_loop(0, FPAIRS, forward_pair, 0, unroll=4)

    ROWS = TILE // Q

    def farthest(d, q):
        return 8 if (d == 0) == (q % 2 == 0) else 7

    def zat(d, dist):
        return (z + dist) % NZ if d == 0 else (z - dist + NZ) % NZ

    def zto(d, step=1):
        return dev(dz=step if d == 0 else -step)

    def sum_hop(dist):
        step = 2 - dist % 2
        for q in range(Q):
            part = pl.ds(q * ROWS, ROWS)
            for d in (0, 1):
                far = farthest(d, q)
                if dist > far:
                    continue
                term = fout[table[F_LAST, zat(d, dist)], part, :]
                if step == 2 and dist < 8:
                    term = term.astype(F32)
                    for other in (dist + 1, dist + 2):
                        if other <= far:
                            wait(zr.at[d, other - 1, part], zs_recv.at[d, other - 1, q])
                            term = term + zr[d, other - 1, part, :].astype(F32)
                    term = term.astype(BF)
                zs[d, dist - 1, part, :] = term
                send(
                    zs.at[d, dist - 1, part], zr.at[d, dist - 1, part], zs_send, zs_recv.at[d, dist - 1, q], zto(d, step)
                )

    for dist in (8, 7, 5, 6, 3, 4, 1, 2):
        sum_hop(dist)
    totals = []
    for q in range(Q):
        part = pl.ds(q * ROWS, ROWS)
        total = fout[table[F_LAST, z], part, :].astype(F32)
        for d in (0, 1):
            for slot in (0, 1):
                wait(zr.at[d, slot, part], zs_recv.at[d, slot, q])
                total = total + zr[d, slot, part, :].astype(F32)
        totals.append(total.astype(BF))
    agg = jnp.concatenate(totals, axis=0)

    w = wv[...]
    pre = jnp.dot(agg, w, preferred_element_type=F32)
    sig = jax.nn.sigmoid(pre)
    grad_pre = (cv[...].astype(F32) * sig * (1.0 + pre * (1.0 - sig))).astype(BF)
    grad_agg = lax.dot_general(w, grad_pre, (((1,), (1,)), ((), ())), preferred_element_type=F32).astype(BF)
    gts = (gt0, gt1)
    for h in (0, 1):
        gts[h][z] = grad_agg[128 * h : 128 * h + 128]

    FR = F // Q

    def halves(h):
        return [(pl.ds(k * FR, FR), h * Q // 2 + k, d) for k in range(Q // 2) for d in (0, 1)]

    def gather_from(dist, h):
        for part, q, d in halves(h):
            ref = gts[h].at[zat(1 - d, dist), part]
            if dist > 0:
                wait(ref, zg_recv.at[d, dist - 1, q])
            for step in (2, 1):
                if dist + step <= farthest(d, q):
                    send(ref, ref, zg_send, zg_recv.at[d, dist + step - 1, q], zto(d, step))

    def gather_end(h):
        for dist in (1, 3, 5, 7, 8):
            for part, q, d in halves(h):
                if dist <= farthest(d, q):
                    wait(gts[h].at[zat(1 - d, dist), part], zg_recv.at[d, dist - 1, q])

    gather_from(0, 0)
    gather_from(0, 1)
    hv[...] = (pre * sig).astype(BF)
    hidden_copy = pltpu.make_async_copy(hv, hidden_o, out_sem.at[0])
    hidden_copy.start()

    def w_stage1():
        lw[...] = lax.dot_general(agg, grad_pre, (((0,), (0,)), ((), ())), preferred_element_type=F32)
        for k in range(4):
            w1s[k] = lw[pl.ds(64 * k, 64), :].astype(BF)
        for k in (1, 2, 3):
            send(w1s.at[(y + k) % NY], w1r.at[k - 1], w_send.at[0], w_recv.at[0], dev(dy=k))

    def w_stage2():
        wait(w1r, w_recv.at[0])
        total = lw[pl.ds(pl.multiple_of(64 * y, 64), 64), :]
        for k in range(3):
            total = total + w1r[k].astype(F32)
        for k in range(4):
            w2s[k] = total[16 * k : 16 * k + 16, :].astype(BF)
        for k in (1, 2, 3):
            send(w2s.at[(x + k) % NX], w2r.at[k - 1], w_send.at[1], w_recv.at[1], dev(dx=k))

    def w_stage3():
        wait(w2r, w_recv.at[1])
        total = w2s[x].astype(F32)
        for k in range(3):
            total = total + w2r[k].astype(F32)
        w3s[0] = total[:, :128].astype(BF)
        w3s[1] = total[:, 128:].astype(BF)
        send(w3s.at[1 - core], w3r, w_send.at[2], w_recv.at[2], dev(flip=1))

    def w_stage4():
        wait(w3r, w_recv.at[2])
        w4[zi] = (w3s[core].astype(F32) + w3r[...].astype(F32)).astype(BF)
        for k in (1, 2, 3):
            send(w4.at[zi], w4.at[zi], w_send.at[3], w_recv.at[3], dev(zz=zq * 4 + (zi + k) % 4))

    def sum4(ref):
        total = ref[0].astype(F32)
        for k in (1, 2, 3):
            total = total + ref[k].astype(F32)
        return total.astype(BF)

    def w_stage5():
        wait(w4.at[pl.ds(0, 3)], w_recv.at[3])
        w5[zq] = sum4(w4)
        for d in (0, 1):
            send(w5.at[zq], w5.at[zq], w_send.at[4], w_recv.at[4 + d], zto(d, 4))

    def w_stage6():
        for d in (0, 1):
            wait(w5.at[(zq + 3 + 2 * d) % 4], w_recv.at[4 + d])
        send(w5.at[(zq + 3) % 4], w5.at[(zq + 3) % 4], w_send.at[5], w_recv.at[6], dev(dz=4))

    def w_stage7():
        wait(w5.at[(zq + 2) % 4], w_recv.at[6])
        w6[core] = sum4(w5)
        send(w6.at[core], w6.at[core], w_send.at[6], w_recv.at[7], dev(flip=1))

    def w_stage8():
        wait(w6.at[1 - core], w_recv.at[7])
        w7[x] = w6[...]
        for k in (1, 2, 3):
            send(w7.at[x], w7.at[x], w_send.at[7], w_recv.at[8], dev(dx=k))

    def w_stage9():
        wait(w7.at[pl.ds(0, 3)], w_recv.at[8])
        w8[y] = w7[...]
        for k in (1, 2, 3):
            send(w8.at[y], w8.at[y], w_send.at[8], w_recv.at[9], dev(dy=k))

    def w_stage10():
        wait(w8.at[pl.ds(0, 3)], w_recv.at[9])
        scale = (TILE * NX * NY * NZ * 2) ** -0.5
        for i in range(4):
            for j in range(4):
                for k in range(2):
                    gwv[pl.ds(64 * i + 16 * j, 16), pl.ds(128 * k, 128)] = w8[i, j, k].astype(F32) * scale
        gw_copy = pltpu.make_async_copy(gwv, gw_o, out_sem.at[1])
        gw_copy.start()
        return gw_copy

    w_stage1()
    gather_from(2, 0)
    gather_from(2, 1)
    w_stage2()
    gather_from(4, 0)
    gather_from(4, 1)
    w_stage3()
    gather_from(6, 0)
    gather_from(6, 1)
    w_stage4()
    gather_end(0)
    w_stage5()

    def products(h, first, end):
        half = pl.ds(128 * h, 128)

        def backward_pair(q, carry):
            a = jnp.concatenate([gts[h][table[B_OTH, 2 * q]], gts[h][table[B_OTH, 2 * q + 1]]], axis=1)
            b = jnp.concatenate([av[table[B_IDX, 2 * q]], av[table[B_IDX, 2 * q + 1]]], axis=0)
            keep = table[B_KEEP, 2 * q].astype(F32)
            total = gfv[half, :] * keep + jnp.dot(a, b, preferred_element_type=F32)
            gfv[half, :] = total
            bout[q, half, :] = total.astype(BF)
            return carry

        if first == 0:
            gfv[half, :] = jnp.zeros((128, TILE), F32)
        lax.fori_loop(first, end, backward_pair, 0, unroll=4)

    def term(u, g, e, flip=0):
        dx, dy = (e, g) if u % 2 == 0 else (g, e)
        c = 8 * ((y + dy) % NY) + 2 * ((x + dx) % NX) + (core + flip) % 2
        return bout[table[B_LAST, c], pl.ds(64 * u, 64), :]

    def to_u(u, da, db):
        return dev(dx=db, dy=da) if u % 2 == 0 else dev(dx=da, dy=db)

    def to_sibling(h):
        for g in range(4):
            for u in (2 * h, 2 * h + 1):
                for e in range(4):
                    sib_s[u, g, e] = term(u, REL[g], REL[e], 1)
                send(sib_s.at[u, g], sib_r.at[u, g], sb_send, sb_recv.at[u, g], dev(flip=1))

    def both(u, g, e):
        return term(u, REL[g], REL[e]).astype(F32) + sib_r[u, g, e].astype(F32)

    def first_axis(h):
        for g in range(3):
            for u in (2 * h, 2 * h + 1):
                wait(sib_r.at[u, g], sb_recv.at[u, g])
                for e in range(4):
                    ps[u, g, e] = both(u, g, e).astype(BF)
                send(ps.at[u, g], pr.at[u, g], rp_send.at[0], rp_recv.at[u, g], to_u(u, REL[g], 0))

    def second_axis(h):
        for u in (2 * h, 2 * h + 1):
            wait(sib_r.at[u, 3], sb_recv.at[u, 3])
            for g in range(3):
                wait(pr.at[u, g], rp_recv.at[u, g])
            for e in range(4):
                total = both(u, 3, e)
                for g in range(3):
                    total = total + pr[u, g, e].astype(F32)
                if e < 3:
                    qs[u, e] = total.astype(BF)
                    send(qs.at[u, e], qr.at[u, e], rp_send.at[1], rp_recv.at[u, 3 + e], to_u(u, 0, REL[e]))
                else:
                    vv[u] = total

    def last_sum(h):
        for u in (2 * h, 2 * h + 1):
            total = vv[u]
            for e in range(3):
                wait(qr.at[u, e], rp_recv.at[u, 3 + e])
                total = total + qr[u, e].astype(F32)
            gft[pl.ds(64 * u, 64), :] = total

    MID = BPAIRS // 2
    products(0, 0, BPAIRS)
    to_sibling(0)
    w_stage6()
    gather_end(1)
    products(1, 0, MID)
    first_axis(0)
    products(1, MID, BPAIRS)
    to_sibling(1)
    w_stage7()
    first_axis(1)
    w_stage8()
    second_axis(0)
    w_stage9()
    second_axis(1)
    last_sum(0)
    gw_copy = w_stage10()
    last_sum(1)
    hv2 = xg.at[NCOLS]
    hv2[...] = jnp.transpose(gft[...]).astype(BF)
    gf_copy = pltpu.make_async_copy(hv2, gf_o, out_sem.at[2])
    gf_copy.start()
    hidden_copy.wait()
    gw_copy.wait()
    gf_copy.wait()
    wait(xg.at[pl.ds(0, NCOLS - 1)], ag_send)
    wait(xg.at[pl.ds(0, NZ - 1)], zs_send)
    wait(xg.at[pl.ds(0, NZ - 1)], zg_send)
    wait(sib_s, sb_send)
    wait(ps, rp_send.at[0])
    wait(qs, rp_send.at[1])
    wait(w1r, w_send.at[0])
    wait(w2r, w_send.at[1])
    wait(w3r, w_send.at[2])
    wait(w4.at[pl.ds(0, 3)], w_send.at[3])
    wait(w5.at[pl.ds(0, 2)], w_send.at[4])
    wait(w5.at[0], w_send.at[5])
    wait(w6.at[0], w_send.at[6])
    wait(w7.at[pl.ds(0, 3)], w_send.at[7])
    wait(w8.at[pl.ds(0, 3)], w_send.at[8])


def hand_over(a, b, c, a_o, b_o, c_o, a_v, b_v, c_v, sem):
    trips = [(a, a_v, a_o), (b, b_v, b_o), (c, c_v, c_o)]
    into = [pltpu.make_async_copy(src, via, sem.at[0, k]) for k, (src, via, _) in enumerate(trips)]
    out = [pltpu.make_async_copy(via, dst, sem.at[1, k]) for k, (_, via, dst) in enumerate(trips)]
    for copy in into:
        copy.start()
    for first, second in zip(into, out):
        first.wait()
        second.start()
    for copy in out:
        copy.wait()


def per_device(feats, tile_values, tile_rows, tile_cols, tile_count, weight, cotangent):
    vm, dma = pltpu.VMEM, pltpu.SemaphoreType.DMA
    scratch = [
        vm((1, 1, 1, SLOTS), jnp.int32),
        vm((1, 1, 1, SLOTS), jnp.int32),
        vm((8, 128), jnp.int32),
        vm((8, 128), jnp.int32),
        pltpu.SMEM((8, 128), jnp.int32),
        vm((SLOTS, TILE, TILE), BF),
        vm((NCOLS + 1, TILE, F), BF),
        vm((FPAIRS + 1, TILE, F), BF),
        vm((TILE, F), F32),
        vm((F, F), BF),
        vm((TILE, F), BF),
        vm((2, 8, TILE, F), BF),
        vm((2, 8, TILE, F), BF),
        vm((NZ + 1, F // 2, TILE), BF),
        vm((NZ + 1, F // 2, TILE), BF),
        vm((BPAIRS + 1, F, TILE), BF),
        vm((4, 4, 4, 64, TILE), BF),
        vm((4, 4, 4, 64, TILE), BF),
        vm((4, 3, 4, 64, TILE), BF),
        vm((4, 3, 4, 64, TILE), BF),
        vm((4, 3, 64, TILE), BF),
        vm((4, 3, 64, TILE), BF),
        vm((4, 64, TILE), F32),
        vm((F, TILE), F32),
        vm((F, TILE), F32),
        vm((TILE, F), BF),
        vm((4, 64, F), BF),
        vm((3, 64, F), BF),
        vm((4, 16, F), BF),
        vm((3, 16, F), BF),
        vm((2, 16, 128), BF),
        vm((16, 128), BF),
        vm((4, 16, 128), BF),
        vm((4, 16, 128), BF),
        vm((2, 16, 128), BF),
        vm((4, 2, 16, 128), BF),
        vm((4, 4, 2, 16, 128), BF),
        vm((F, F), F32),
        vm((F, F), F32),
        dma((8,)),
        dma,
        dma((2, 31)),
        dma,
        dma((2, 8, Q)),
        dma,
        dma((2, 8, Q)),
        dma,
        dma((4, 4)),
        dma((2,)),
        dma((4, 6)),
        dma((9,)),
        dma((10,)),
        dma((3,)),
    ]
    any_spec = pl.BlockSpec(memory_space=pltpu.HBM)
    results = pl.pallas_call(
        kernel,
        out_shape=(
            jax.ShapeDtypeStruct((TILE, F), BF),
            jax.ShapeDtypeStruct((TILE, F), BF),
            jax.ShapeDtypeStruct((F, F), F32),
        ),
        in_specs=[pl.BlockSpec(memory_space=pltpu.VMEM)] + [any_spec] * 6,
        out_specs=(any_spec,) * 3,
        scratch_shapes=scratch,
        compiler_params=pltpu.CompilerParams(
            collective_id=0, has_side_effects=True, vmem_limit_bytes=60 * 1024 * 1024
        ),
        cost_estimate=pl.CostEstimate(flops=2_000_000_000, bytes_accessed=4_000_000, transcendentals=32768),
    )(tile_count, tile_rows, tile_cols, feats, tile_values, weight, cotangent)
    return pl.pallas_call(
        hand_over,
        out_shape=[jax.ShapeDtypeStruct(a.shape, a.dtype) for a in results],
        in_specs=[any_spec] * 3,
        out_specs=[any_spec] * 3,
        scratch_shapes=[vm(a.shape, a.dtype) for a in results] + [dma((2, 3))],
        cost_estimate=pl.CostEstimate(flops=0, bytes_accessed=800_000, transcendentals=0),
        compiler_params=pltpu.CompilerParams(vmem_limit_bytes=60 * 1024 * 1024),
    )(*results)


def solution(mesh):
    return jax.shard_map(
        per_device,
        mesh=mesh,
        in_specs=(
            P(("row", "col", "depth"), None),
            P("row", "col", "depth", None, None, None),
            P("row", "col", "depth", None),
            P("row", "col", "depth", None),
            P("row", "col", "depth"),
            P(),
            P(("row", "col", "depth"), None),
        ),
        out_specs=(P(("row", "col", "depth"), None), P(("row", "col", "depth"), None), P()),
        check_vma=False,
    )
```

```python
import jax
import jax.numpy as jnp
from jax import lax
from jax.experimental import pallas as pl
from jax.experimental.pallas import tpu as pltpu
from jax.sharding import PartitionSpec as P

MESH = pl.DeviceIdType.MESH
BF, F32 = jnp.bfloat16, jnp.float32

NX, NY, NZ = 4, 4, 16
TILE, F, SLOTS = 128, 256, 96
NROWS, NCOLS = NZ, NX * NY * 2
FPOS, BPOS = SLOTS + NROWS, SLOTS + NCOLS
FPAIRS, BPAIRS = FPOS // 2, BPOS // 2
Q = 2
REL = (2, 1, 3, 0)

F_IDX, F_OTH, F_KEEP, F_LAST, B_IDX, B_OTH, B_KEEP, B_LAST, F_OTH_B = range(9)


def schedule(keys, others, count, zero, none):
    full = (128, 128)
    lane, sub = lax.broadcasted_iota(jnp.int32, full, 1), lax.broadcasted_iota(jnp.int32, full, 0)

    def down(ref):
        return jnp.transpose(jnp.broadcast_to(ref, full))

    key = jnp.broadcast_to(keys, full)
    key_down = jnp.transpose(key)
    live = lane < count
    same = (key == key_down) & (sub < lane) & (sub < count)
    rank = jnp.sum(jnp.where(same, 1, 0), axis=0, keepdims=True)
    hot = (key == sub) & live
    number = jnp.sum(jnp.where(hot, 1, 0), axis=1, keepdims=True)
    padded = jnp.broadcast_to(lax.shift_left(lax.shift_right_logical(number + 1, 1), 1), full)
    place = rank + jnp.sum(jnp.where(sub < key, padded, 0), axis=0, keepdims=True)
    place = jnp.where(live, jnp.broadcast_to(place, full), 1000)
    at = jnp.transpose(place) == lane
    slot = jnp.sum(jnp.where(at, sub, 0), axis=0, keepdims=True)
    other = jnp.sum(jnp.where(at, down(others) - zero, 0), axis=0, keepdims=True) + zero
    keep = 1 - jnp.sum(jnp.where(at & (down(rank) == 0), 1, 0), axis=0, keepdims=True)
    last = jnp.max(jnp.where(hot, lax.shift_right_logical(place, 1), -1), axis=1, keepdims=True)
    last = down_first(jnp.where(number > 0, last, none), full)
    return [slot, other, keep, last]


def down_first(column, full):
    return jnp.transpose(jnp.broadcast_to(column, full))[:1]


def wait(ref, sem):
    pltpu.make_async_copy(ref, ref, sem).wait()


def kernel(
    counts, rows_i, cols_i, feats, tiles, weight, cot, hidden_o, gf_o, gw_o,
    rows_v, cols_v, pad, table_v, table, av, xa, xb, fout, wv, cv, zs, zr, gt0, gt1, bout, sib_s, sib_r,
    ps, pr, qs, qr, vv, gft, gfv, hv, gf_v,
    w1s, w1r, w2s, w2r, w3s, w3r, w4, w5, w7, w8, lw, gwv,
    loc, ag_send, ag_recv, zs_send, zs_recv, zg_send, zg_recv,
    sb_send, sb_recv, rp_send, rp_recv, w_send, w_recv, out_sem,
):
    row, z, depth = lax.axis_index("row"), lax.axis_index("col"), lax.axis_index("depth")
    y, x, core = row // 2, (row % 2) * 2 + depth // 2, depth % 2

    def dev(dx=0, dy=0, dz=0, flip=0, zz=None):
        nx, ny = (x + dx) % NX, (y + dy) % NY
        nz = (z + dz + NZ) % NZ if zz is None else zz
        nc = (core + flip) % 2
        return {"row": ny * 2 + nx // 2, "col": nz, "depth": (nx % 2) * 2 + nc}

    def send(src, dst, ssem, rsem, to):
        pltpu.make_async_remote_copy(
            src_ref=src, dst_ref=dst, send_sem=ssem, recv_sem=rsem, device_id=to, device_id_type=MESH
        ).start()

    zi, zq = z % 4, z // 4
    partners = [dev(flip=1)] + [dev(dz=step) for step in (1, -1, 2, -2, 4, -4)]
    for k in (1, 2, 3):
        partners += [dev(dx=k), dev(dy=k), dev(zz=zq * 4 + (zi + k) % 4)]
    barrier = pltpu.get_barrier_semaphore()
    for to in partners:
        pl.semaphore_signal(barrier, inc=1, device_id=to, device_id_type=MESH)

    xs = (xa, xb)
    mine = (16 * core + 4 * y + x, 16 * core + 4 * x + y)
    local = []
    for k, (src, dst) in enumerate(
        [(rows_i, rows_v), (cols_i, cols_v), (tiles.at[0, 0, 0], av), (weight, wv), (cot, cv)]
        + [(feats.at[pl.ds(64 * h, 64)], xs[h].at[mine[h]]) for h in (0, 1)]
    ):
        local.append(pltpu.make_async_copy(src, dst, loc.at[k]))
        local[k].start()
    pl.semaphore_wait(barrier, len(partners))

    def to_ab(h, da, db):
        return dev(dx=da, dy=db) if h == 0 else dev(dx=db, dy=da)

    along = ((x, y), (y, x))

    def xpart(h, da, db):
        return xs[h].at[16 * core + 4 * ((along[h][1] + db) % 4) + (along[h][0] + da) % 4]

    def xline(h, db, flip=0):
        return xs[h].at[pl.ds(16 * ((core + flip) % 2) + 4 * ((along[h][1] + db) % 4), 4)]

    def own(h, da, db, k):
        send(feats.at[pl.ds(64 * h, 64)], xpart(h, 0, 0), ag_send.at[h], ag_recv.at[h, k], to_ab(h, da, db))

    def to_sib(h, db):
        send(xline(h, db), xline(h, db), ag_send.at[h], ag_recv.at[h, 15 + db], dev(flip=1))

    for k in (2, 1, 3):
        for h in (0, 1):
            own(h, k, 0, k - 1)
    for k in (2, 1, 3):
        for h in (0, 1):
            own(h, 0, k, 2 + k)

    for part in xs:
        part[NCOLS] = jnp.zeros((TILE // 2, F), BF)
    for part in (gt0, gt1):
        part[NZ] = jnp.zeros((F // 2, TILE), BF)
    fout[FPAIRS] = jnp.zeros((TILE, F), BF)
    bout[BPAIRS] = jnp.zeros((F, TILE), BF)
    pad[...] = jnp.zeros_like(pad)
    local[0].wait()
    local[1].wait()
    pad[0:1, 0:SLOTS] = rows_v[0, 0]
    pad[1:2, 0:SLOTS] = cols_v[0, 0]
    live_count = jnp.broadcast_to(counts[0], (128, 128))
    by_row = schedule(pad[0:1], pad[1:2], live_count, NCOLS, FPAIRS)
    by_col = schedule(pad[1:2], pad[0:1], live_count, NZ, BPAIRS)
    piece = by_row[1]
    py, px, pc = lax.shift_right_logical(piece, 3), lax.shift_right_logical(piece, 1) & 3, piece & 1
    by_row[1] = jnp.where(piece < NCOLS, 16 * pc + 4 * py + px, NCOLS)
    by_x = jnp.where(piece < NCOLS, 16 * pc + 4 * px + py, NCOLS)
    for k, line in enumerate(by_row + by_col + [by_x]):
        table_v[k : k + 1, :] = line
    table_copy = pltpu.make_async_copy(table_v, table, loc.at[7])
    table_copy.start()

    local[5].wait()
    local[6].wait()
    for k in (1, 3, 2):
        for h in (0, 1):
            wait(xpart(h, 4 - k, 0), ag_recv.at[h, k - 1])
            src = xpart(h, 4 - k, 0)
            for kb in (2, 1, 3):
                send(src, src, ag_send.at[h], ag_recv.at[h, 3 + 3 * (4 - k) + kb - 1], to_ab(h, 0, kb))
    for h in (0, 1):
        to_sib(h, 0)
    for k in (1, 3, 2):
        for h in (0, 1):
            for e in (0, 3, 1, 2):
                wait(xpart(h, e, 4 - k), ag_recv.at[h, 3 + 3 * e + k - 1])
            to_sib(h, 4 - k)
    for h in (0, 1):
        for db in (0, 3, 1, 2):
            wait(xline(h, db, 1), ag_recv.at[h, 15 + db])
    for copy in local[2:5]:
        copy.wait()
    table_copy.wait()

    def forward_pair(q, carry):
        a = jnp.concatenate([av[table[F_IDX, 2 * q]], av[table[F_IDX, 2 * q + 1]]], axis=1)
        halves_of = [(xa, F_OTH, 0), (xb, F_OTH_B, 0), (xa, F_OTH, 1), (xb, F_OTH_B, 1)]
        b = jnp.concatenate([part[table[line, 2 * q + k]] for part, line, k in halves_of], axis=0)
        keep = table[F_KEEP, 2 * q].astype(F32)
        total = carry * keep + jnp.dot(a, b, preferred_element_type=F32)
        fout[q] = total.astype(BF)
        return total

    lax.fori_loop(0, FPAIRS, forward_pair, jnp.zeros((TILE, F), F32), unroll=14)

    ROWS = TILE // Q

    def farthest(d, q):
        return 8 if (d == 0) == (q % 2 == 0) else 7

    def zat(d, dist):
        return (z + dist) % NZ if d == 0 else (z - dist + NZ) % NZ

    def zto(d, step=1):
        return dev(dz=step if d == 0 else -step)

    def sum_hop(dist):
        step = 2 - dist % 2
        for q in range(Q):
            part = pl.ds(q * ROWS, ROWS)
            for d in (0, 1):
                far = farthest(d, q)
                if dist > far:
                    continue
                term = fout[table[F_LAST, zat(d, dist)], part, :]
                if step == 2 and dist < 8:
                    term = term.astype(F32)
                    for other in (dist + 1, dist + 2):
                        if other <= far:
                            wait(zr.at[d, other - 1, part], zs_recv.at[d, other - 1, q])
                            term = term + zr[d, other - 1, part, :].astype(F32)
                    term = term.astype(BF)
                zs[d, dist - 1, part, :] = term
                send(
                    zs.at[d, dist - 1, part], zr.at[d, dist - 1, part], zs_send, zs_recv.at[d, dist - 1, q], zto(d, step)
                )

    for dist in (8, 7, 5, 6, 3, 4, 1, 2):
        sum_hop(dist)
    totals = []
    for q in range(Q):
        part = pl.ds(q * ROWS, ROWS)
        total = fout[table[F_LAST, z], part, :].astype(F32)
        for d in (0, 1):
            for slot in (0, 1):
                wait(zr.at[d, slot, part], zs_recv.at[d, slot, q])
                total = total + zr[d, slot, part, :].astype(F32)
        totals.append(total.astype(BF))
    agg = jnp.concatenate(totals, axis=0)

    w = wv[...]
    pre = jnp.dot(agg, w, preferred_element_type=F32)
    sig = jax.nn.sigmoid(pre)
    grad_pre = (cv[...].astype(F32) * sig * (1.0 + pre * (1.0 - sig))).astype(BF)
    grad_agg = lax.dot_general(w, grad_pre, (((1,), (1,)), ((), ())), preferred_element_type=F32).astype(BF)
    gts = (gt0, gt1)
    for h in (0, 1):
        gts[h][z] = grad_agg[128 * h : 128 * h + 128]

    FR = F // Q

    def halves(h):
        return [(pl.ds(k * FR, FR), h * Q // 2 + k, d) for k in range(Q // 2) for d in (0, 1)]

    def gather_from(dist, h):
        for part, q, d in halves(h):
            ref = gts[h].at[zat(1 - d, dist), part]
            if dist > 0:
                wait(ref, zg_recv.at[d, dist - 1, q])
            for step in (2, 1):
                if dist + step <= farthest(d, q):
                    send(ref, ref, zg_send, zg_recv.at[d, dist + step - 1, q], zto(d, step))

    def gather_end(h):
        for dist in (1, 3, 5, 7, 8):
            for part, q, d in halves(h):
                if dist <= farthest(d, q):
                    wait(gts[h].at[zat(1 - d, dist), part], zg_recv.at[d, dist - 1, q])

    gather_from(0, 0)
    hv[...] = (pre * sig).astype(BF)
    hidden_copy = pltpu.make_async_copy(hv, hidden_o, out_sem.at[0])
    hidden_copy.start()

    def w_stage1():
        lw[...] = lax.dot_general(agg, grad_pre, (((0,), (0,)), ((), ())), preferred_element_type=F32)
        for k in range(4):
            w1s[k] = lw[pl.ds(64 * k, 64), :].astype(BF)
        for k in (1, 2, 3):
            send(w1s.at[(y + k) % NY], w1r.at[k - 1], w_send.at[0], w_recv.at[0], dev(dy=k))

    def w_stage2():
        wait(w1r, w_recv.at[0])
        total = lw[pl.ds(pl.multiple_of(64 * y, 64), 64), :]
        for k in range(3):
            total = total + w1r[k].astype(F32)
        for k in range(4):
            w2s[k] = total[16 * k : 16 * k + 16, :].astype(BF)
        for k in (1, 2, 3):
            send(w2s.at[(x + k) % NX], w2r.at[k - 1], w_send.at[1], w_recv.at[1], dev(dx=k))

    def w_stage3():
        wait(w2r, w_recv.at[1])
        total = w2s[x].astype(F32)
        for k in range(3):
            total = total + w2r[k].astype(F32)
        w3s[...] = total.astype(BF)
        send(w3s, w3r, w_send.at[2], w_recv.at[2], dev(flip=1))

    def w_stage4():
        wait(w3r, w_recv.at[2])
        w4[zi] = (w3s[...].astype(F32) + w3r[...].astype(F32)).astype(BF)
        for k in (1, 2, 3):
            send(w4.at[zi], w4.at[zi], w_send.at[3], w_recv.at[3], dev(zz=zq * 4 + (zi + k) % 4))

    def sum4(ref):
        total = ref[0].astype(F32)
        for k in (1, 2, 3):
            total = total + ref[k].astype(F32)
        return total.astype(BF)

    def w_stage5():
        wait(w4.at[pl.ds(0, 3)], w_recv.at[3])
        w5[zq] = sum4(w4)
        for d in (0, 1):
            send(w5.at[zq], w5.at[zq], w_send.at[4], w_recv.at[4 + d], zto(d, 4))

    def w_stage6():
        for d in (0, 1):
            wait(w5.at[(zq + 3 + 2 * d) % 4], w_recv.at[4 + d])
        send(w5.at[(zq + 3) % 4], w5.at[(zq + 3) % 4], w_send.at[5], w_recv.at[6], dev(dz=4))

    def w_stage7():
        wait(w5.at[(zq + 2) % 4], w_recv.at[6])
        w7[x] = sum4(w5)
        for k in (1, 2, 3):
            send(w7.at[x], w7.at[x], w_send.at[7], w_recv.at[8], dev(dx=k))

    def w_stage8():
        wait(w7.at[pl.ds(0, 3)], w_recv.at[8])
        w8[y] = w7[...]
        for k in (1, 2, 3):
            send(w8.at[y], w8.at[y], w_send.at[8], w_recv.at[9], dev(dy=k))

    def w_stage9():
        wait(w8.at[pl.ds(0, 3)], w_recv.at[9])
        scale = (TILE * NX * NY * NZ * 2) ** -0.5
        for i in range(4):
            for j in range(4):
                gwv[pl.ds(64 * i + 16 * j, 16), :] = w8[i, j].astype(F32) * scale
        gw_copy = pltpu.make_async_copy(gwv, gw_o, out_sem.at[1])
        gw_copy.start()
        return gw_copy

    w_stage1()
    gather_from(2, 0)
    gather_from(0, 1)
    w_stage2()
    gather_from(4, 0)
    gather_from(2, 1)
    w_stage3()
    gather_from(6, 0)
    gather_from(4, 1)
    w_stage4()
    gather_end(0)

    def products(h, first, end):
        half = pl.ds(128 * h, 128)

        def backward_pair(q, carry):
            a = jnp.concatenate([gts[h][table[B_OTH, 2 * q]], gts[h][table[B_OTH, 2 * q + 1]]], axis=1)
            b = jnp.concatenate([av[table[B_IDX, 2 * q]], av[table[B_IDX, 2 * q + 1]]], axis=0)
            keep = table[B_KEEP, 2 * q].astype(F32)
            total = carry * keep + jnp.dot(a, b, preferred_element_type=F32)
            bout[q, half, :] = total.astype(BF)
            return total

        begin = jnp.zeros((128, TILE), F32) if first == 0 else gfv[half, :]
        gfv[half, :] = lax.fori_loop(first, end, backward_pair, begin, unroll=16)

    def term(u, g, e, flip=0):
        dx, dy = (e, g) if u % 2 == 0 else (g, e)
        c = 8 * ((y + dy) % NY) + 2 * ((x + dx) % NX) + (core + flip) % 2
        return bout[table[B_LAST, c], pl.ds(64 * u, 64), :]

    def to_u(u, da, db):
        return dev(dx=db, dy=da) if u % 2 == 0 else dev(dx=da, dy=db)

    def to_sibling(h):
        for g in range(4):
            for u in (2 * h, 2 * h + 1):
                for e in range(4):
                    sib_s[u, g, e] = term(u, REL[g], REL[e], 1)
                send(sib_s.at[u, g], sib_r.at[u, g], sb_send, sb_recv.at[u, g], dev(flip=1))

    def both(u, g, e):
        return term(u, REL[g], REL[e]).astype(F32) + sib_r[u, g, e].astype(F32)

    def first_axis(h):
        for g in range(3):
            for u in (2 * h, 2 * h + 1):
                wait(sib_r.at[u, g], sb_recv.at[u, g])
                for e in range(4):
                    ps[u, g, e] = both(u, g, e).astype(BF)
                send(ps.at[u, g], pr.at[u, g], rp_send.at[0], rp_recv.at[u, g], to_u(u, REL[g], 0))

    def second_axis(h):
        for u in (2 * h, 2 * h + 1):
            wait(sib_r.at[u, 3], sb_recv.at[u, 3])
            for g in range(3):
                wait(pr.at[u, g], rp_recv.at[u, g])
            for e in range(4):
                total = both(u, 3, e)
                for g in range(3):
                    total = total + pr[u, g, e].astype(F32)
                if e < 3:
                    qs[u, e] = total.astype(BF)
                    send(qs.at[u, e], qr.at[u, e], rp_send.at[1], rp_recv.at[u, 3 + e], to_u(u, 0, REL[e]))
                else:
                    vv[u] = total

    def last_sum(h):
        for u in (2 * h, 2 * h + 1):
            total = vv[u]
            for e in range(3):
                wait(qr.at[u, e], rp_recv.at[u, 3 + e])
                total = total + qr[u, e].astype(F32)
            gft[pl.ds(64 * u, 64), :] = total

    MID = BPAIRS // 2
    products(0, 0, MID)
    gather_from(6, 1)
    w_stage5()
    products(0, MID, BPAIRS)
    to_sibling(0)
    gather_end(1)
    products(1, 0, MID)
    first_axis(0)
    w_stage6()
    products(1, MID, BPAIRS)
    to_sibling(1)
    first_axis(1)
    w_stage7()
    second_axis(0)
    second_axis(1)
    w_stage8()
    last_sum(0)
    last_sum(1)
    gf_v[...] = jnp.transpose(gft[...]).astype(BF)
    gf_copy = pltpu.make_async_copy(gf_v, gf_o, out_sem.at[2])
    gf_copy.start()
    gw_copy = w_stage9()
    hidden_copy.wait()
    gw_copy.wait()
    gf_copy.wait()
    for h in (0, 1):
        wait(xs[h].at[pl.ds(0, NCOLS - 1)], ag_send.at[h])
    wait(fout.at[pl.ds(0, NZ - 1)], zs_send)
    wait(fout.at[pl.ds(0, NZ - 1)], zg_send)
    wait(sib_s, sb_send)
    wait(ps, rp_send.at[0])
    wait(qs, rp_send.at[1])
    wait(w1r, w_send.at[0])
    wait(w2r, w_send.at[1])
    wait(w3r, w_send.at[2])
    wait(w4.at[pl.ds(0, 3)], w_send.at[3])
    wait(w5.at[pl.ds(0, 2)], w_send.at[4])
    wait(w5.at[0], w_send.at[5])
    wait(w7.at[pl.ds(0, 3)], w_send.at[7])
    wait(w8.at[pl.ds(0, 3)], w_send.at[8])


def hand_over(a, b, c, a_o, b_o, c_o, a_v, b_v, c_v, sem):
    trips = [(a, a_v, a_o), (b, b_v, b_o), (c, c_v, c_o)]
    into = [pltpu.make_async_copy(src, via, sem.at[0, k]) for k, (src, via, _) in enumerate(trips)]
    out = [pltpu.make_async_copy(via, dst, sem.at[1, k]) for k, (_, via, dst) in enumerate(trips)]
    for copy in into:
        copy.start()
    for first, second in zip(into, out):
        first.wait()
        second.start()
    for copy in out:
        copy.wait()


def per_device(feats, tile_values, tile_rows, tile_cols, tile_count, weight, cotangent):
    vm, dma = pltpu.VMEM, pltpu.SemaphoreType.DMA
    scratch = [
        vm((1, 1, 1, SLOTS), jnp.int32),
        vm((1, 1, 1, SLOTS), jnp.int32),
        vm((8, 128), jnp.int32),
        vm((16, 128), jnp.int32),
        pltpu.SMEM((16, 128), jnp.int32),
        vm((SLOTS, TILE, TILE), BF),
        vm((NCOLS + 1, TILE // 2, F), BF),
        vm((NCOLS + 1, TILE // 2, F), BF),
        vm((FPAIRS + 1, TILE, F), BF),
        vm((F, F), BF),
        vm((TILE, F), BF),
        vm((2, 8, TILE, F), BF),
        vm((2, 8, TILE, F), BF),
        vm((NZ + 1, F // 2, TILE), BF),
        vm((NZ + 1, F // 2, TILE), BF),
        vm((BPAIRS + 1, F, TILE), BF),
        vm((4, 4, 4, 64, TILE), BF),
        vm((4, 4, 4, 64, TILE), BF),
        vm((4, 3, 4, 64, TILE), BF),
        vm((4, 3, 4, 64, TILE), BF),
        vm((4, 3, 64, TILE), BF),
        vm((4, 3, 64, TILE), BF),
        vm((4, 64, TILE), F32),
        vm((F, TILE), F32),
        vm((F, TILE), F32),
        vm((TILE, F), BF),
        vm((TILE, F), BF),
        vm((4, 64, F), BF),
        vm((3, 64, F), BF),
        vm((4, 16, F), BF),
        vm((3, 16, F), BF),
        vm((16, F), BF),
        vm((16, F), BF),
        vm((4, 16, F), BF),
        vm((4, 16, F), BF),
        vm((4, 16, F), BF),
        vm((4, 4, 16, F), BF),
        vm((F, F), F32),
        vm((F, F), F32),
        dma((8,)),
        dma((2,)),
        dma((2, 19)),
        dma,
        dma((2, 8, Q)),
        dma,
        dma((2, 8, Q)),
        dma,
        dma((4, 4)),
        dma((2,)),
        dma((4, 6)),
        dma((9,)),
        dma((10,)),
        dma((3,)),
    ]
    any_spec = pl.BlockSpec(memory_space=pltpu.HBM)
    results = pl.pallas_call(
        kernel,
        out_shape=(
            jax.ShapeDtypeStruct((TILE, F), BF),
            jax.ShapeDtypeStruct((TILE, F), BF),
            jax.ShapeDtypeStruct((F, F), F32),
        ),
        in_specs=[pl.BlockSpec(memory_space=pltpu.VMEM)] + [any_spec] * 6,
        out_specs=(any_spec,) * 3,
        scratch_shapes=scratch,
        compiler_params=pltpu.CompilerParams(
            collective_id=0, has_side_effects=True, vmem_limit_bytes=60 * 1024 * 1024
        ),
        cost_estimate=pl.CostEstimate(flops=2_000_000_000, bytes_accessed=4_000_000, transcendentals=32768),
    )(tile_count, tile_rows, tile_cols, feats, tile_values, weight, cotangent)
    return pl.pallas_call(
        hand_over,
        out_shape=[jax.ShapeDtypeStruct(a.shape, a.dtype) for a in results],
        in_specs=[any_spec] * 3,
        out_specs=[any_spec] * 3,
        scratch_shapes=[vm(a.shape, a.dtype) for a in results] + [dma((2, 3))],
        cost_estimate=pl.CostEstimate(flops=0, bytes_accessed=800_000, transcendentals=0),
        compiler_params=pltpu.CompilerParams(vmem_limit_bytes=60 * 1024 * 1024),
    )(*results)


def solution(mesh):
    return jax.shard_map(
        per_device,
        mesh=mesh,
        in_specs=(
            P(("row", "col", "depth"), None),
            P("row", "col", "depth", None, None, None),
            P("row", "col", "depth", None),
            P("row", "col", "depth", None),
            P("row", "col", "depth"),
            P(),
            P(("row", "col", "depth"), None),
        ),
        out_specs=(P(("row", "col", "depth"), None), P(("row", "col", "depth"), None), P()),
        check_vma=False,
    )
```

```python
import jax
import jax.numpy as jnp
from jax import lax
from jax.experimental import pallas as pl
from jax.experimental.pallas import tpu as pltpu
from jax.sharding import PartitionSpec as P

MESH = pl.DeviceIdType.MESH
BF, F32 = jnp.bfloat16, jnp.float32

NX, NY, NZ = 4, 4, 16
TILE, F, SLOTS = 128, 256, 96
NROWS, NCOLS = NZ, NX * NY * 2
FPOS, BPOS = SLOTS + NROWS, SLOTS + NCOLS
FPAIRS, BPAIRS = FPOS // 2, BPOS // 2
Q = 4
REL = (2, 1, 3, 0)

F_IDX, F_OTH, F_KEEP, F_LAST, B_IDX, B_OTH, B_KEEP, B_LAST, F_OTH_B = range(9)


def schedule(keys, others, count, zero, none):
    full = (128, 128)
    lane, sub = lax.broadcasted_iota(jnp.int32, full, 1), lax.broadcasted_iota(jnp.int32, full, 0)

    def down(ref):
        return jnp.transpose(jnp.broadcast_to(ref, full))

    key = jnp.broadcast_to(keys, full)
    key_down = jnp.transpose(key)
    live = lane < count
    same = (key == key_down) & (sub < lane) & (sub < count)
    rank = jnp.sum(jnp.where(same, 1, 0), axis=0, keepdims=True)
    hot = (key == sub) & live
    number = jnp.sum(jnp.where(hot, 1, 0), axis=1, keepdims=True)
    padded = jnp.broadcast_to(lax.shift_left(lax.shift_right_logical(number + 1, 1), 1), full)
    place = rank + jnp.sum(jnp.where(sub < key, padded, 0), axis=0, keepdims=True)
    place = jnp.where(live, jnp.broadcast_to(place, full), 1000)
    at = jnp.transpose(place) == lane
    slot = jnp.sum(jnp.where(at, sub, 0), axis=0, keepdims=True)
    other = jnp.sum(jnp.where(at, down(others) - zero, 0), axis=0, keepdims=True) + zero
    keep = 1 - jnp.sum(jnp.where(at & (down(rank) == 0), 1, 0), axis=0, keepdims=True)
    last = jnp.max(jnp.where(hot, lax.shift_right_logical(place, 1), -1), axis=1, keepdims=True)
    last = down_first(jnp.where(number > 0, last, none), full)
    return [slot, other, keep, last]


def down_first(column, full):
    return jnp.transpose(jnp.broadcast_to(column, full))[:1]


def wait(ref, sem):
    pltpu.make_async_copy(ref, ref, sem).wait()


def kernel(
    counts, rows_i, cols_i, feats, tiles, weight, cot, hidden_o, gf_o, gw_o,
    rows_v, cols_v, pad, table_v, table, av, xa, xb, fout, wv, cv, zs, zr, gt0, gt1, bout, sib_s, sib_r,
    ps, pr, qs, qr, vv, gft, gfv, hv, gf_v,
    w1s, w1r, w2s, w2r, w3s, w3r, w4, w5, w7, w8, lw, gwv,
    loc, ag_send, ag_recv, zs_send, zs_recv, zg_send, zg_recv,
    sb_send, sb_recv, rp_send, rp_recv, w_send, w_recv, out_sem,
):
    row, z, depth = lax.axis_index("row"), lax.axis_index("col"), lax.axis_index("depth")
    y, x, core = row // 2, (row % 2) * 2 + depth // 2, depth % 2

    def dev(dx=0, dy=0, dz=0, flip=0, zz=None):
        nx, ny = (x + dx) % NX, (y + dy) % NY
        nz = (z + dz + NZ) % NZ if zz is None else zz
        nc = (core + flip) % 2
        return {"row": ny * 2 + nx // 2, "col": nz, "depth": (nx % 2) * 2 + nc}

    def send(src, dst, ssem, rsem, to):
        pltpu.make_async_remote_copy(
            src_ref=src, dst_ref=dst, send_sem=ssem, recv_sem=rsem, device_id=to, device_id_type=MESH
        ).start()

    zi, zq = z % 4, z // 4
    partners = [dev(flip=1)] + [dev(dz=step) for step in (1, -1, 2, -2, 4, -4)]
    for k in (1, 2, 3):
        partners += [dev(dx=k), dev(dy=k), dev(zz=zq * 4 + (zi + k) % 4)]
    barrier = pltpu.get_barrier_semaphore()
    for to in partners:
        pl.semaphore_signal(barrier, inc=1, device_id=to, device_id_type=MESH)

    xs = (xa, xb)
    mine = (16 * core + 4 * y + x, 16 * core + 4 * x + y)
    local = []
    for k, (src, dst) in enumerate(
        [(rows_i, rows_v), (cols_i, cols_v), (tiles.at[0, 0, 0], av), (weight, wv), (cot, cv)]
        + [(feats.at[pl.ds(64 * h, 64)], xs[h].at[mine[h]]) for h in (0, 1)]
    ):
        local.append(pltpu.make_async_copy(src, dst, loc.at[k]))
        local[k].start()
    pl.semaphore_wait(barrier, len(partners))

    def to_ab(h, da, db):
        return dev(dx=da, dy=db) if h == 0 else dev(dx=db, dy=da)

    along = ((x, y), (y, x))

    def xpart(h, da, db):
        return xs[h].at[16 * core + 4 * ((along[h][1] + db) % 4) + (along[h][0] + da) % 4]

    def xline(h, db, flip=0):
        return xs[h].at[pl.ds(16 * ((core + flip) % 2) + 4 * ((along[h][1] + db) % 4), 4)]

    def own(h, da, db, k):
        send(feats.at[pl.ds(64 * h, 64)], xpart(h, 0, 0), ag_send.at[h], ag_recv.at[h, k], to_ab(h, da, db))

    def to_sib(h, db):
        send(xline(h, db), xline(h, db), ag_send.at[h], ag_recv.at[h, 15 + db], dev(flip=1))

    for k in (2, 1, 3):
        for h in (0, 1):
            own(h, k, 0, k - 1)
    for k in (2, 1, 3):
        for h in (0, 1):
            own(h, 0, k, 2 + k)

    for part in xs:
        part[NCOLS] = jnp.zeros((TILE // 2, F), BF)
    for part in (gt0, gt1):
        part[NZ] = jnp.zeros((F // 2, TILE), BF)
    fout[FPAIRS] = jnp.zeros((TILE, F), BF)
    bout[BPAIRS] = jnp.zeros((F, TILE), BF)
    pad[...] = jnp.zeros_like(pad)
    local[0].wait()
    local[1].wait()
    pad[0:1, 0:SLOTS] = rows_v[0, 0]
    pad[1:2, 0:SLOTS] = cols_v[0, 0]
    live_count = jnp.broadcast_to(counts[0], (128, 128))
    by_row = schedule(pad[0:1], pad[1:2], live_count, NCOLS, FPAIRS)
    by_col = schedule(pad[1:2], pad[0:1], live_count, NZ, BPAIRS)
    piece = by_row[1]
    py, px, pc = lax.shift_right_logical(piece, 3), lax.shift_right_logical(piece, 1) & 3, piece & 1
    by_row[1] = jnp.where(piece < NCOLS, 16 * pc + 4 * py + px, NCOLS)
    by_x = jnp.where(piece < NCOLS, 16 * pc + 4 * px + py, NCOLS)
    for k, line in enumerate(by_row + by_col + [by_x]):
        table_v[k : k + 1, :] = line
    table_copy = pltpu.make_async_copy(table_v, table, loc.at[7])
    table_copy.start()

    local[5].wait()
    local[6].wait()
    for k in (1, 3, 2):
        for h in (0, 1):
            wait(xpart(h, 4 - k, 0), ag_recv.at[h, k - 1])
            src = xpart(h, 4 - k, 0)
            for kb in (2, 1, 3):
                send(src, src, ag_send.at[h], ag_recv.at[h, 3 + 3 * (4 - k) + kb - 1], to_ab(h, 0, kb))
    for h in (0, 1):
        to_sib(h, 0)
    for k in (1, 3, 2):
        for h in (0, 1):
            for e in (0, 3, 1, 2):
                wait(xpart(h, e, 4 - k), ag_recv.at[h, 3 + 3 * e + k - 1])
            to_sib(h, 4 - k)
    for h in (0, 1):
        for db in (0, 3, 1, 2):
            wait(xline(h, db, 1), ag_recv.at[h, 15 + db])
    for copy in local[2:5]:
        copy.wait()
    table_copy.wait()

    def forward_pair(q, carry):
        a = jnp.concatenate([av[table[F_IDX, 2 * q]], av[table[F_IDX, 2 * q + 1]]], axis=1)
        halves_of = [(xa, F_OTH, 0), (xb, F_OTH_B, 0), (xa, F_OTH, 1), (xb, F_OTH_B, 1)]
        b = jnp.concatenate([part[table[line, 2 * q + k]] for part, line, k in halves_of], axis=0)
        keep = table[F_KEEP, 2 * q].astype(F32)
        total = carry * keep + jnp.dot(a, b, preferred_element_type=F32)
        fout[q] = total.astype(BF)
        return total

    lax.fori_loop(0, FPAIRS, forward_pair, jnp.zeros((TILE, F), F32), unroll=14)

    ROWS = TILE // Q

    def farthest(d, q):
        return 8 if (d == 0) == (q % 2 == 0) else 7

    def zat(d, dist):
        return (z + dist) % NZ if d == 0 else (z - dist + NZ) % NZ

    def zto(d, step=1):
        return dev(dz=step if d == 0 else -step)

    def sum_hop(dist):
        step = 2 - dist % 2
        for q in range(Q):
            part = pl.ds(q * ROWS, ROWS)
            for d in (0, 1):
                far = farthest(d, q)
                if dist > far:
                    continue
                term = fout[table[F_LAST, zat(d, dist)], part, :]
                if step == 2 and dist < 8:
                    term = term.astype(F32)
                    for other in (dist + 1, dist + 2):
                        if other <= far:
                            wait(zr.at[d, other - 1, part], zs_recv.at[d, other - 1, q])
                            term = term + zr[d, other - 1, part, :].astype(F32)
                    term = term.astype(BF)
                zs[d, dist - 1, part, :] = term
                send(
                    zs.at[d, dist - 1, part], zr.at[d, dist - 1, part], zs_send, zs_recv.at[d, dist - 1, q], zto(d, step)
                )

    for dist in (8, 7, 5, 6, 3, 4, 1, 2):
        sum_hop(dist)
    totals = []
    for q in range(Q):
        part = pl.ds(q * ROWS, ROWS)
        total = fout[table[F_LAST, z], part, :].astype(F32)
        for d in (0, 1):
            for slot in (0, 1):
                wait(zr.at[d, slot, part], zs_recv.at[d, slot, q])
                total = total + zr[d, slot, part, :].astype(F32)
        totals.append(total.astype(BF))
    agg = jnp.concatenate(totals, axis=0)

    w = wv[...]
    pre = jnp.dot(agg, w, preferred_element_type=F32)
    sig = jax.nn.sigmoid(pre)
    grad_pre = (cv[...].astype(F32) * sig * (1.0 + pre * (1.0 - sig))).astype(BF)
    grad_agg = lax.dot_general(w, grad_pre, (((1,), (1,)), ((), ())), preferred_element_type=F32).astype(BF)
    gts = (gt0, gt1)
    for h in (0, 1):
        gts[h][z] = grad_agg[128 * h : 128 * h + 128]

    FR = F // Q

    def halves(h):
        return [(pl.ds(k * FR, FR), h * Q // 2 + k, d) for k in range(Q // 2) for d in (0, 1)]

    def gather_from(dist, h):
        for part, q, d in halves(h):
            ref = gts[h].at[zat(1 - d, dist), part]
            if dist > 0:
                wait(ref, zg_recv.at[d, dist - 1, q])
            for step in (2, 1):
                if dist + step <= farthest(d, q):
                    send(ref, ref, zg_send, zg_recv.at[d, dist + step - 1, q], zto(d, step))

    def gather_end(h):
        for dist in (1, 3, 5, 7, 8):
            for part, q, d in halves(h):
                if dist <= farthest(d, q):
                    wait(gts[h].at[zat(1 - d, dist), part], zg_recv.at[d, dist - 1, q])

    gather_from(0, 0)
    hv[...] = (pre * sig).astype(BF)
    hidden_copy = pltpu.make_async_copy(hv, hidden_o, out_sem.at[0])
    hidden_copy.start()

    def w_stage1():
        lw[...] = lax.dot_general(agg, grad_pre, (((0,), (0,)), ((), ())), preferred_element_type=F32)
        for k in range(4):
            w1s[k] = lw[pl.ds(64 * k, 64), :].astype(BF)
        for k in (1, 2, 3):
            send(w1s.at[(y + k) % NY], w1r.at[k - 1], w_send.at[0], w_recv.at[0], dev(dy=k))

    def w_stage2():
        wait(w1r, w_recv.at[0])
        total = lw[pl.ds(pl.multiple_of(64 * y, 64), 64), :]
        for k in range(3):
            total = total + w1r[k].astype(F32)
        for k in range(4):
            w2s[k] = total[16 * k : 16 * k + 16, :].astype(BF)
        for k in (1, 2, 3):
            send(w2s.at[(x + k) % NX], w2r.at[k - 1], w_send.at[1], w_recv.at[1], dev(dx=k))

    def w_stage3():
        wait(w2r, w_recv.at[1])
        total = w2s[x].astype(F32)
        for k in range(3):
            total = total + w2r[k].astype(F32)
        w3s[...] = total.astype(BF)
        send(w3s, w3r, w_send.at[2], w_recv.at[2], dev(flip=1))

    def w_stage4():
        wait(w3r, w_recv.at[2])
        w4[zi] = (w3s[...].astype(F32) + w3r[...].astype(F32)).astype(BF)
        for k in (1, 2, 3):
            send(w4.at[zi], w4.at[zi], w_send.at[3], w_recv.at[3], dev(zz=zq * 4 + (zi + k) % 4))

    def sum4(ref):
        total = ref[0].astype(F32)
        for k in (1, 2, 3):
            total = total + ref[k].astype(F32)
        return total.astype(BF)

    def w_stage5():
        wait(w4.at[pl.ds(0, 3)], w_recv.at[3])
        w5[zq] = sum4(w4)
        for d in (0, 1):
            send(w5.at[zq], w5.at[zq], w_send.at[4], w_recv.at[4 + d], zto(d, 4))

    def w_stage6():
        for d in (0, 1):
            wait(w5.at[(zq + 3 + 2 * d) % 4], w_recv.at[4 + d])
        send(w5.at[(zq + 3) % 4], w5.at[(zq + 3) % 4], w_send.at[5], w_recv.at[6], dev(dz=4))

    def w_stage7():
        wait(w5.at[(zq + 2) % 4], w_recv.at[6])
        w7[x] = sum4(w5)
        for k in (1, 2, 3):
            send(w7.at[x], w7.at[x], w_send.at[7], w_recv.at[8], dev(dx=k))

    def w_stage8():
        wait(w7.at[pl.ds(0, 3)], w_recv.at[8])
        w8[y] = w7[...]
        for k in (1, 2, 3):
            send(w8.at[y], w8.at[y], w_send.at[8], w_recv.at[9], dev(dy=k))

    def w_stage9():
        wait(w8.at[pl.ds(0, 3)], w_recv.at[9])
        scale = (TILE * NX * NY * NZ * 2) ** -0.5
        for i in range(4):
            for j in range(4):
                gwv[pl.ds(64 * i + 16 * j, 16), :] = w8[i, j].astype(F32) * scale
        gw_copy = pltpu.make_async_copy(gwv, gw_o, out_sem.at[1])
        gw_copy.start()
        return gw_copy

    w_stage1()
    gather_from(2, 0)
    gather_from(0, 1)
    w_stage2()
    gather_from(4, 0)
    gather_from(2, 1)
    w_stage3()
    gather_from(6, 0)
    gather_from(4, 1)
    w_stage4()
    gather_end(0)

    def products(h, first, end):
        half = pl.ds(128 * h, 128)

        def backward_pair(q, carry):
            a = jnp.concatenate([gts[h][table[B_OTH, 2 * q]], gts[h][table[B_OTH, 2 * q + 1]]], axis=1)
            b = jnp.concatenate([av[table[B_IDX, 2 * q]], av[table[B_IDX, 2 * q + 1]]], axis=0)
            keep = table[B_KEEP, 2 * q].astype(F32)
            total = carry * keep + jnp.dot(a, b, preferred_element_type=F32)
            bout[q, half, :] = total.astype(BF)
            return total

        begin = jnp.zeros((128, TILE), F32) if first == 0 else gfv[half, :]
        gfv[half, :] = lax.fori_loop(first, end, backward_pair, begin, unroll=16)

    def term(u, g, e, flip=0):
        dx, dy = (e, g) if u % 2 == 0 else (g, e)
        c = 8 * ((y + dy) % NY) + 2 * ((x + dx) % NX) + (core + flip) % 2
        return bout[table[B_LAST, c], pl.ds(64 * u, 64), :]

    def to_u(u, da, db):
        return dev(dx=db, dy=da) if u % 2 == 0 else dev(dx=da, dy=db)

    def to_sibling(h):
        for g in range(4):
            for u in (2 * h, 2 * h + 1):
                for e in range(4):
                    sib_s[u, g, e] = term(u, REL[g], REL[e], 1)
                send(sib_s.at[u, g], sib_r.at[u, g], sb_send, sb_recv.at[u, g], dev(flip=1))

    def both(u, g, e):
        return term(u, REL[g], REL[e]).astype(F32) + sib_r[u, g, e].astype(F32)

    def first_axis(h):
        for g in range(3):
            for u in (2 * h, 2 * h + 1):
                wait(sib_r.at[u, g], sb_recv.at[u, g])
                for e in range(4):
                    ps[u, g, e] = both(u, g, e).astype(BF)
                send(ps.at[u, g], pr.at[u, g], rp_send.at[0], rp_recv.at[u, g], to_u(u, REL[g], 0))

    def second_axis(h):
        for u in (2 * h, 2 * h + 1):
            wait(sib_r.at[u, 3], sb_recv.at[u, 3])
            for g in range(3):
                wait(pr.at[u, g], rp_recv.at[u, g])
            for e in range(4):
                total = both(u, 3, e)
                for g in range(3):
                    total = total + pr[u, g, e].astype(F32)
                if e < 3:
                    qs[u, e] = total.astype(BF)
                    send(qs.at[u, e], qr.at[u, e], rp_send.at[1], rp_recv.at[u, 3 + e], to_u(u, 0, REL[e]))
                else:
                    vv[u] = total

    def last_sum(h):
        for u in (2 * h, 2 * h + 1):
            total = vv[u]
            for e in range(3):
                wait(qr.at[u, e], rp_recv.at[u, 3 + e])
                total = total + qr[u, e].astype(F32)
            gft[pl.ds(64 * u, 64), :] = total

    MID = BPAIRS // 2
    products(0, 0, MID)
    gather_from(6, 1)
    w_stage5()
    products(0, MID, BPAIRS)
    to_sibling(0)
    gather_end(1)
    products(1, 0, MID)
    first_axis(0)
    w_stage6()
    products(1, MID, BPAIRS)
    to_sibling(1)
    first_axis(1)
    w_stage7()
    second_axis(0)
    second_axis(1)
    w_stage8()
    last_sum(0)
    last_sum(1)
    gf_v[...] = jnp.transpose(gft[...]).astype(BF)
    gf_copy = pltpu.make_async_copy(gf_v, gf_o, out_sem.at[2])
    gf_copy.start()
    gw_copy = w_stage9()
    hidden_copy.wait()
    gw_copy.wait()
    gf_copy.wait()
    for h in (0, 1):
        wait(xs[h].at[pl.ds(0, NCOLS - 1)], ag_send.at[h])
    wait(fout.at[pl.ds(0, NZ - 1)], zs_send)
    wait(fout.at[pl.ds(0, NZ - 1)], zg_send)
    wait(sib_s, sb_send)
    wait(ps, rp_send.at[0])
    wait(qs, rp_send.at[1])
    wait(w1r, w_send.at[0])
    wait(w2r, w_send.at[1])
    wait(w3r, w_send.at[2])
    wait(w4.at[pl.ds(0, 3)], w_send.at[3])
    wait(w5.at[pl.ds(0, 2)], w_send.at[4])
    wait(w5.at[0], w_send.at[5])
    wait(w7.at[pl.ds(0, 3)], w_send.at[7])
    wait(w8.at[pl.ds(0, 3)], w_send.at[8])


def hand_over(a, b, c, a_o, b_o, c_o, a_v, b_v, c_v, sem):
    trips = [(a, a_v, a_o), (b, b_v, b_o), (c, c_v, c_o)]
    into = [pltpu.make_async_copy(src, via, sem.at[0, k]) for k, (src, via, _) in enumerate(trips)]
    out = [pltpu.make_async_copy(via, dst, sem.at[1, k]) for k, (_, via, dst) in enumerate(trips)]
    for copy in into:
        copy.start()
    for first, second in zip(into, out):
        first.wait()
        second.start()
    for copy in out:
        copy.wait()


def per_device(feats, tile_values, tile_rows, tile_cols, tile_count, weight, cotangent):
    vm, dma = pltpu.VMEM, pltpu.SemaphoreType.DMA
    scratch = [
        vm((1, 1, 1, SLOTS), jnp.int32),
        vm((1, 1, 1, SLOTS), jnp.int32),
        vm((8, 128), jnp.int32),
        vm((16, 128), jnp.int32),
        pltpu.SMEM((16, 128), jnp.int32),
        vm((SLOTS, TILE, TILE), BF),
        vm((NCOLS + 1, TILE // 2, F), BF),
        vm((NCOLS + 1, TILE // 2, F), BF),
        vm((FPAIRS + 1, TILE, F), BF),
        vm((F, F), BF),
        vm((TILE, F), BF),
        vm((2, 8, TILE, F), BF),
        vm((2, 8, TILE, F), BF),
        vm((NZ + 1, F // 2, TILE), BF),
        vm((NZ + 1, F // 2, TILE), BF),
        vm((BPAIRS + 1, F, TILE), BF),
        vm((4, 4, 4, 64, TILE), BF),
        vm((4, 4, 4, 64, TILE), BF),
        vm((4, 3, 4, 64, TILE), BF),
        vm((4, 3, 4, 64, TILE), BF),
        vm((4, 3, 64, TILE), BF),
        vm((4, 3, 64, TILE), BF),
        vm((4, 64, TILE), F32),
        vm((F, TILE), F32),
        vm((F, TILE), F32),
        vm((TILE, F), BF),
        vm((TILE, F), BF),
        vm((4, 64, F), BF),
        vm((3, 64, F), BF),
        vm((4, 16, F), BF),
        vm((3, 16, F), BF),
        vm((16, F), BF),
        vm((16, F), BF),
        vm((4, 16, F), BF),
        vm((4, 16, F), BF),
        vm((4, 16, F), BF),
        vm((4, 4, 16, F), BF),
        vm((F, F), F32),
        vm((F, F), F32),
        dma((8,)),
        dma((2,)),
        dma((2, 19)),
        dma,
        dma((2, 8, Q)),
        dma,
        dma((2, 8, Q)),
        dma,
        dma((4, 4)),
        dma((2,)),
        dma((4, 6)),
        dma((9,)),
        dma((10,)),
        dma((3,)),
    ]
    any_spec = pl.BlockSpec(memory_space=pltpu.HBM)
    results = pl.pallas_call(
        kernel,
        out_shape=(
            jax.ShapeDtypeStruct((TILE, F), BF),
            jax.ShapeDtypeStruct((TILE, F), BF),
            jax.ShapeDtypeStruct((F, F), F32),
        ),
        in_specs=[pl.BlockSpec(memory_space=pltpu.VMEM)] + [any_spec] * 6,
        out_specs=(any_spec,) * 3,
        scratch_shapes=scratch,
        compiler_params=pltpu.CompilerParams(
            collective_id=0, has_side_effects=True, vmem_limit_bytes=60 * 1024 * 1024
        ),
        cost_estimate=pl.CostEstimate(flops=2_000_000_000, bytes_accessed=4_000_000, transcendentals=32768),
    )(tile_count, tile_rows, tile_cols, feats, tile_values, weight, cotangent)
    return pl.pallas_call(
        hand_over,
        out_shape=[jax.ShapeDtypeStruct(a.shape, a.dtype) for a in results],
        in_specs=[any_spec] * 3,
        out_specs=[any_spec] * 3,
        scratch_shapes=[vm(a.shape, a.dtype) for a in results] + [dma((2, 3))],
        cost_estimate=pl.CostEstimate(flops=0, bytes_accessed=800_000, transcendentals=0),
        compiler_params=pltpu.CompilerParams(vmem_limit_bytes=60 * 1024 * 1024),
    )(*results)


def solution(mesh):
    return jax.shard_map(
        per_device,
        mesh=mesh,
        in_specs=(
            P(("row", "col", "depth"), None),
            P("row", "col", "depth", None, None, None),
            P("row", "col", "depth", None),
            P("row", "col", "depth", None),
            P("row", "col", "depth"),
            P(),
            P(("row", "col", "depth"), None),
        ),
        out_specs=(P(("row", "col", "depth"), None), P(("row", "col", "depth"), None), P()),
        check_vma=False,
    )
```
